32 devices in a mesh: groups: 2 (over x), visit: 16 (over z, y, core).
Axes of the slice: x: 2, y: 2, z: 4, core: 2. Of those that a mesh axis runs over, the one named last changes fastest.
Arguments:
- science: float32 [8192, 1024], P(('groups', 'visit')), parts along dimension 0, may hold values from -6 to 6
- template: bfloat16 [8192, 1024], P(('groups', 'visit')), parts along dimension 0, may hold values from -6 to 6
- owner_map: int32 [32], P('groups'), parts along dimension 0, may hold values from 0 to 15, as said below
- covering: int32 [32, 4], P(('groups', 'visit')), parts along dimension 0, may hold values from 0 to 15, as said below
- row_shift: int32 [32, 4], P(('groups', 'visit')), parts along dimension 0, may hold values from -128 to 128, as said below
- col_shift: int32 [32, 4], P(('groups', 'visit')), parts along dimension 0, may hold values from -256 to 256, as said below
- basis_cols: float32 [20, 21], replicated, may hold values from -1.25 to 1.25
- basis_rows: float32 [20, 21], replicated, may hold values from -1.25 to 1.25
- coeffs: float32 [8, 20], P('groups'), parts along dimension 0, may hold values from -1.25 to 1.25
- psf_kernel: float32 [9, 9], replicated, may hold values from 0 to 0.25
Outputs:
- difference: float32 [8192, 1024], P(('groups', 'visit')), parts along dimension 0
- detection: float32 [8192, 1024], P(('groups', 'visit')), parts along dimension 0
The draws below stay inside these ranges and needn't reach their ends.
There are 2 independent parts, one for each index of `groups`. The reference program is written for one: setup_inputs(seed, part) draws one part's arguments, and reference() takes and returns one part's arrays. A program takes and returns all parts, laid end to end along the dimension named above; an argument that names none is the same for every part. Nothing has to cross between parts.
Inputs may be any that keep to these rules, and one draw needn't show every extreme that they name: owner_map is a permutation: every device stores exactly one template piece. `covering`: the 4 pieces listed for a row block are different; the first is the piece stored on that block's own device; every listed piece is stored on a device at most 3 positions away along the visit axis, and on some device exactly 3. `row_shift`: the first slot of every row block has shift 0; both ends of the range are reached. `col_shift`: the first slot of every row block has shift 0; both ends of the range are reached.
All inputs are finite; a program needn't handle non-finite values.
Results may differ from the reference program's by a relative error of at most 0.005.
Values may be sent and summed in bfloat16 or wider, within the bound.
A program may use at most 64 MiB of HBM per device.

```python
import jax
import jax.numpy as jnp
from jax import lax

NB = 20
KS = 21
RIM = 10
KP = 9
PR = 4
ROWS = 256
COLS = 1024
PIECES = 4
SLOTS = 4
REACH = 3
VISITS = 4
IMAGE_ROWS = 4096
N_VISIT = 16


def layout_draw(key):
    base_key = jax.random.fold_in(key, 71)
    owner_table = jax.random.permutation(jax.random.fold_in(base_key, 1), N_VISIT).astype(jnp.int32)
    stored = jnp.argsort(owner_table, stable=True).astype(jnp.int32)
    device = jnp.arange(N_VISIT, dtype=jnp.int32)
    steps_list = jnp.concatenate([jnp.arange(-REACH, 0, dtype=jnp.int32), jnp.arange(1, REACH + 1, dtype=jnp.int32)])
    target = device[:, None] + steps_list[None, :]
    inside_axis = (target >= 0) & (target < N_VISIT)
    position_rank = jnp.arange(2 * REACH, dtype=jnp.int32)
    raw_score = jax.random.randint(jax.random.fold_in(base_key, 2), (N_VISIT, 2 * REACH), 0, 4096, dtype=jnp.int32)
    scores = jnp.where(inside_axis, raw_score * (2 * REACH) + position_rank[None, :], 4096 * 2 * REACH + position_rank[None, :])
    picked = lax.top_k(-scores, SLOTS - 1)[1]
    chosen = jnp.take_along_axis(target, picked, axis=1)
    devices = jnp.concatenate([device[:, None], chosen], axis=1)
    pieces = stored[devices]
    return (owner_table, pieces.astype(jnp.int32))


def draw_owner_map(key, part):
    return layout_draw(key)[0]


def draw_covering(key, part):
    return layout_draw(key)[1]


def shift_draw(key, limit, salt):
    values = jax.random.randint(jax.random.fold_in(key, salt), (N_VISIT, SLOTS), -limit, limit + 1, dtype=jnp.int32)
    values = values.at[:, 0].set(0)
    chosen = jax.random.randint(jax.random.fold_in(key, salt + 1), (), 0, N_VISIT, dtype=jnp.int32)
    values = values.at[chosen, 1].set(limit)
    values = values.at[chosen, 2].set(-limit)
    return values


def draw_row_shift(key, part):
    return shift_draw(key, ROWS // 2, 81)


def draw_col_shift(key, part):
    return shift_draw(key, COLS // 4, 91)


def block_levels(own_key, extent, cuts, low, largest):
    factor_of = 1.0
    for position, parts in cuts:
        steps = jax.random.uniform(jax.random.fold_in(jax.random.fold_in(own_key, 6), position), (parts,), jnp.float32, low / len(cuts), largest / len(cuts))
        factor_of = factor_of * jnp.repeat(jnp.exp(steps), extent[position] // parts).reshape((-1,) + (1,) * (len(extent) - 1 - position))
    return factor_of


def bell_draw(rng, dims, deviation, reach, cuts=(), kind=jnp.bfloat16):
    values = jax.random.normal(rng, dims, jnp.float32) * deviation
    if len(cuts) > 0:
        values = block_levels(rng, dims, cuts, -0.22, 0.18) * values
    return jnp.clip(values, min=-reach, max=reach).astype(kind)


def setup_inputs(seed: int = 0, part: int = 0) -> dict:
    streams_of = jax.random.split(jax.random.key(seed), 11)
    part_keys = jax.random.split(jax.random.fold_in(streams_of[10], part), 11)
    science = bell_draw(part_keys[0], (IMAGE_ROWS, COLS), 1.0, 6.0, ((0, 16),), jnp.float32)
    template = bell_draw(part_keys[1], (IMAGE_ROWS, COLS), 1.0, 6.0, ((0, 16),))
    owner_map = draw_owner_map(jax.random.fold_in(jax.random.fold_in(streams_of[10], part), 71), part)
    covering = draw_covering(jax.random.fold_in(jax.random.fold_in(streams_of[10], part), 71), part)
    row_shift = draw_row_shift(jax.random.fold_in(jax.random.fold_in(streams_of[10], part), 71), part)
    col_shift = draw_col_shift(jax.random.fold_in(jax.random.fold_in(streams_of[10], part), 71), part)
    basis_cols = bell_draw(streams_of[6], (NB, KS), KS ** -0.5, 1.25, (), jnp.float32)
    basis_rows = bell_draw(streams_of[7], (NB, KS), KS ** -0.5, 1.25, (), jnp.float32)
    coeffs = bell_draw(part_keys[8], (VISITS, NB), NB ** -0.5, 1.25, (), jnp.float32)
    psf_kernel = jnp.clip(jax.random.uniform(streams_of[9], (KP, KP), jnp.float32, 0.0, 0.25), 0.0, 0.25)
    return {"science": science, "template": template, "owner_map": owner_map, "covering": covering, "row_shift": row_shift, "col_shift": col_shift, "basis_cols": basis_cols, "basis_rows": basis_rows, "coeffs": coeffs, "psf_kernel": psf_kernel}


def round_trip(values):
    return lax.optimization_barrier(values.astype(jnp.bfloat16)).astype(jnp.float32)

def place_piece(piece, row_off, col_off):
    half_rows = ROWS // 2
    quarter_cols = COLS // 4
    padded = jnp.pad(piece, ((half_rows, half_rows), (quarter_cols, quarter_cols)))
    start_row = (half_rows - row_off).astype(jnp.int32)
    start_col = (quarter_cols - col_off).astype(jnp.int32)
    return lax.dynamic_slice(padded, (start_row, start_col), (ROWS, COLS))

def reference(science, template, owner_map, covering, row_shift, col_shift, basis_cols, basis_rows, coeffs, psf_kernel):
    stored = template.reshape(N_VISIT, ROWS, COLS)
    ones_piece = jnp.ones((ROWS, COLS), jnp.float32)

    def canvas_of(device):
        placed_sum = jnp.zeros((ROWS, COLS), jnp.float32)
        coverage = jnp.zeros((ROWS, COLS), jnp.float32)
        for slot_index in range(SLOTS):
            holder = owner_map[covering[device, slot_index]].astype(jnp.int32)
            piece = lax.dynamic_index_in_dim(stored, holder, 0, keepdims=False).astype(jnp.float32)
            placed_sum = placed_sum + place_piece(piece, row_shift[device, slot_index], col_shift[device, slot_index])
            coverage = coverage + place_piece(ones_piece, row_shift[device, slot_index], col_shift[device, slot_index])
        return (placed_sum / coverage).astype(jnp.bfloat16)
    canvases = jnp.roll(lax.map(canvas_of, jnp.arange(N_VISIT, dtype=jnp.int32)), 1, axis=0)
    taps_cols = round_trip(basis_cols)
    taps_psf = round_trip(psf_kernel)
    weights_all = round_trip(coeffs[:, :, None] * basis_rows[None, :, :])
    science_visits = jnp.roll(science, ROWS, axis=0).reshape(VISITS, PIECES * ROWS, COLS)
    visit_rows = PIECES * ROWS

    def visit_fn(visit):
        start = (visit * PIECES).astype(jnp.int32)
        image = lax.dynamic_slice_in_dim(canvases, start, PIECES, 0).reshape(visit_rows, COLS).astype(jnp.float32)
        padded = jnp.pad(image, ((RIM, RIM), (RIM, RIM)))
        col_pass = jnp.zeros((NB, visit_rows + 2 * RIM, COLS), jnp.float32)
        for tap_index in range(KS):
            col_pass = col_pass + taps_cols[:, tap_index, None, None] * padded[None, :, tap_index:tap_index + COLS]
        col_pass = round_trip(col_pass)
        weights = lax.dynamic_index_in_dim(weights_all, visit, 0, keepdims=False)
        model_image = jnp.zeros((visit_rows, COLS), jnp.float32)
        for tap_index in range(KS):
            model_image = model_image + jnp.einsum('b,brc->rc', weights[:, tap_index], col_pass[:, tap_index:tap_index + visit_rows], precision=lax.Precision.HIGHEST)
        difference = lax.dynamic_index_in_dim(science_visits, visit, 0, keepdims=False) - model_image
        variance = jnp.mean(difference * difference)
        rounded = jnp.pad(round_trip(difference), ((PR, PR), (PR, PR)))
        response = jnp.zeros((visit_rows, COLS), jnp.float32)
        for row_tap in range(KP):
            for col_tap in range(KP):
                response = response + taps_psf[row_tap, col_tap] * rounded[row_tap:row_tap + visit_rows, col_tap:col_tap + COLS]
        detection = response / jnp.sqrt(variance + 1e-06)
        return (difference, detection)
    differences, detections = lax.map(visit_fn, jnp.arange(VISITS, dtype=jnp.int32))
    differences = jnp.roll(differences.reshape(N_VISIT * ROWS, COLS), -ROWS, axis=0)
    detections = jnp.roll(detections.reshape(N_VISIT * ROWS, COLS), -ROWS, axis=0)
    return (differences, detections)
```

```python
import functools

import jax
import jax.numpy as jnp
from jax import lax
from jax.experimental import pallas as pl
from jax.experimental.pallas import tpu as pltpu
from jax.sharding import PartitionSpec as P

PIECES = 4
REACH = 3
LANES = 128
EDGE = 16
MESH = pl.DeviceIdType.MESH


def kernel(
    devices,
    owner_ref,
    covering_ref,
    row_shift_ref,
    col_shift_ref,
    science_ref,
    template_ref,
    basis_cols_ref,
    basis_rows_ref,
    coeffs_ref,
    psf_ref,
    difference_ref,
    detection_ref,
    slots,
    ext,
    ext_low,
    sci_ext,
    small,
    folded,
    weights,
    psf_weights,
    y_model,
    y_psf,
    diff_ext,
    diff_low,
    partial,
    partials,
    piece_send,
    piece_recv,
    forward_send,
    sci_send,
    sci_recv,
    halo_send,
    halo_recv,
    part_send,
    part_recv,
):
    rows, cols = science_ref.shape
    blocks = cols // LANES
    taps = basis_cols_ref.shape[1]
    basis = basis_cols_ref.shape[0]
    psf_taps = psf_ref.shape[0]
    rim, psf_rim = taps // 2, psf_taps // 2
    f32, bf16 = jnp.float32, jnp.bfloat16

    group = lax.axis_index("groups")
    me = lax.axis_index("visit")
    core = lax.rem(me, 2)
    sibling = me + 1 - 2 * core
    held = lax.rem(me + 1, devices)
    visit = held // PIECES
    pos = lax.rem(held, PIECES)
    before = lax.rem(me + devices - 1, devices)
    after = lax.rem(me + 1, devices)
    far = jnp.where(core == 1, me + REACH, me - REACH)
    has_low, has_high = me >= 2, me + 2 < devices
    has_far = (far >= 0) & (far < devices)
    has_before, has_after = pos > 0, pos < PIECES - 1

    def peer(step):
        return lax.rem(visit * PIECES + lax.rem(pos + step, PIECES) + devices - 1, devices)

    barrier = pltpu.get_barrier_semaphore()

    def greet(device):
        pl.semaphore_signal(barrier, inc=1, device_id=(group, device), device_id_type=MESH)

    greet(sibling)
    for step in range(1, PIECES):
        greet(peer(step))
    pl.when(has_low)(lambda: greet(me - 2))
    pl.when(has_high)(lambda: greet(me + 2))
    pl.when(has_far)(lambda: greet(far))
    expected = (
        PIECES + has_low.astype(jnp.int32) + has_high.astype(jnp.int32) + has_far.astype(jnp.int32)
    )
    pl.semaphore_wait(barrier, expected)

    def remote(src, dst, send, recv, device):
        return pltpu.make_async_remote_copy(
            src_ref=src,
            dst_ref=dst,
            send_sem=send,
            recv_sem=recv,
            device_id=(group, device),
            device_id_type=MESH,
        )

    def piece_copy(src, slot, send, device):
        return remote(src, slots.at[slot], send, piece_recv.at[slot], device)

    far_slot = jnp.where(core == 1, 0, 2 * REACH)
    to_high = piece_copy(template_ref, 1, piece_send.at[0], me + 2)
    to_low = piece_copy(template_ref, 5, piece_send.at[1], me - 2)
    to_far = piece_copy(template_ref, far_slot, piece_send.at[2], far)
    to_sibling = piece_copy(template_ref, 2 + 2 * core, piece_send.at[3], sibling)
    sci_up = remote(
        science_ref.at[pl.ds(0, 8)], sci_ext.at[pl.ds(8 + rows, 8)], sci_send.at[0], sci_recv.at[1], before
    )
    sci_down = remote(
        science_ref.at[pl.ds(rows - 8, 8)], sci_ext.at[pl.ds(0, 8)], sci_send.at[1], sci_recv.at[0], after
    )
    pl.when(has_high)(to_high.start)
    pl.when(has_low)(to_low.start)
    pl.when(has_far)(to_far.start)
    to_sibling.start()
    pl.when(has_before)(sci_up.start)
    pl.when(has_after)(sci_down.start)

    lane = lax.broadcasted_iota(jnp.int32, (LANES, 2 * LANES), 1)
    tap = lax.broadcasted_iota(jnp.int32, (LANES, 2 * LANES), 0)
    reverse = jnp.where(lax.rem(tap + lane, 2 * LANES) == 0, 1.0, 0.0).astype(bf16)
    small[...] = jnp.zeros_like(small)
    small[0, 0:basis, 0:taps] = basis_cols_ref[...]
    small[1, 0:basis, 0:taps] = basis_rows_ref[...]
    small[2, 0:psf_taps, 0:psf_taps] = psf_ref[...]
    small[3, 0:1, 0:basis] = coeffs_ref[pl.ds(visit, 1), :]
    diagonal = lax.broadcasted_iota(jnp.int32, (LANES, LANES), 0) == lax.broadcasted_iota(
        jnp.int32, (LANES, LANES), 1
    )
    coeff_col = jnp.sum(
        jnp.where(diagonal, jnp.broadcast_to(small[3, 0:1, :], (LANES, LANES)), 0.0),
        axis=1,
        keepdims=True,
    )
    row_weights = (coeff_col * small[1]).astype(bf16).astype(f32)
    cols_reversed = jnp.dot(small[0].astype(bf16), reverse, preferred_element_type=f32)
    folded[0] = jnp.dot(
        row_weights.T.astype(bf16), cols_reversed.astype(bf16), preferred_element_type=f32
    )
    folded[1] = jnp.dot(small[2].astype(bf16), reverse, preferred_element_type=f32)

    def band(which, index):
        line = folded[which, pl.ds(index, 1), :]
        spread = jnp.broadcast_to(line, (2 * LANES, 2 * LANES))
        rolled = pltpu.roll(spread, 0, 1, stride=1, stride_axis=0)
        return rolled[:, :LANES].astype(bf16)

    steps = (taps + 7) // 8

    def build(step, carry):
        start = pl.multiple_of(step * (2 * LANES), 2 * LANES)
        for s in range(8):
            weights[pl.ds(start, 2 * LANES), s * LANES : (s + 1) * LANES] = band(0, step * 8 + s)
        return carry

    lax.fori_loop(0, steps, build, 0)
    for s in range(psf_taps):
        psf_weights[:, s * LANES : (s + 1) * LANES] = band(1, s)

    sci_ext[pl.ds(8, rows), :] = science_ref[...]
    sci_ext[pl.ds(rows + 16, 8), :] = jnp.zeros((8, cols), f32)
    ext[pl.ds(rows + 2 * EDGE, EDGE), :] = jnp.zeros((EDGE, ext.shape[1]), bf16)
    slots[REACH] = template_ref[...]

    @pl.when(jnp.logical_not(has_before))
    def _():
        sci_ext[pl.ds(0, 8), :] = jnp.zeros((8, cols), f32)
        ext[pl.ds(0, EDGE), :] = jnp.zeros((EDGE, ext.shape[1]), bf16)

    @pl.when(jnp.logical_not(has_after))
    def _():
        sci_ext[pl.ds(rows + 8, 8), :] = jnp.zeros((8, cols), f32)
        ext[pl.ds(rows + EDGE, EDGE), :] = jnp.zeros((EDGE, ext.shape[1]), bf16)

    from_low = piece_copy(slots.at[1], 2 * core, forward_send.at[0], sibling)
    from_high = piece_copy(slots.at[5], 4 + 2 * core, forward_send.at[1], sibling)

    @pl.when(has_low)
    def _():
        piece_copy(template_ref, 1, piece_send.at[0], sibling).wait_recv()
        from_low.start()

    @pl.when(has_high)
    def _():
        piece_copy(template_ref, 5, piece_send.at[0], sibling).wait_recv()
        from_high.start()

    for slot in (0, 2, 4, 6):
        origin = me + slot - REACH
        pl.when((origin >= 0) & (origin < devices))(
            piece_copy(template_ref, slot, piece_send.at[0], sibling).wait_recv
        )

    row_to = lax.broadcasted_iota(jnp.int32, (rows, rows), 0)
    row_from = lax.broadcasted_iota(jnp.int32, (rows, rows), 1)
    row_line = lax.broadcasted_iota(jnp.int32, (rows, cols), 0)
    col_line = lax.broadcasted_iota(jnp.int32, (rows, cols), 1)
    total = template_ref[...].astype(f32)
    coverage = jnp.ones((rows, cols), f32)
    for k in range(1, covering_ref.shape[1]):
        holder = owner_ref[covering_ref[0, k]]
        row_off, col_off = row_shift_ref[0, k], col_shift_ref[0, k]
        piece = slots[jnp.clip(holder - me + REACH, 0, 2 * REACH)]
        select = jnp.where(row_to - row_from == row_off, 1.0, 0.0).astype(bf16)
        moved = jnp.dot(select, piece, preferred_element_type=f32)
        moved = pltpu.roll(moved, lax.rem(col_off + cols, cols), 1)
        col_old, row_old = col_line - col_off, row_line - row_off
        col_in = (col_old >= 0) & (col_old < cols)
        total = total + jnp.where(col_in, moved, 0.0)
        coverage = coverage + jnp.where(col_in & (row_old >= 0) & (row_old < rows), 1.0, 0.0)
    canvas = total / coverage
    wide = jnp.concatenate([canvas, jnp.zeros((rows, LANES), f32)], axis=1)
    ext[pl.ds(EDGE, rows), :] = pltpu.roll(wide, rim, 1).astype(bf16)

    halo_up = remote(
        ext.at[pl.ds(EDGE, EDGE)], ext.at[pl.ds(rows + EDGE, EDGE)], halo_send.at[0], halo_recv.at[1], before
    )
    halo_down = remote(
        ext.at[pl.ds(rows, EDGE)], ext.at[pl.ds(0, EDGE)], halo_send.at[1], halo_recv.at[0], after
    )
    pl.when(has_before)(halo_up.start)
    pl.when(has_after)(halo_down.start)

    @pl.when(has_before)
    def _():
        halo_down.wait_recv()
        sci_down.wait_recv()

    @pl.when(has_after)
    def _():
        halo_up.wait_recv()
        sci_up.wait_recv()

    ext_low[...] = ext[...].astype(f32)[8 : rows + 2 * EDGE + 8].astype(bf16)
    model_rows = rows + 2 * EDGE
    wide_rows = rows + EDGE
    index = lax.broadcasted_iota(jnp.int32, (wide_rows, LANES), 0)
    low_edge = jnp.where(has_before, 0, psf_rim)
    high_edge = jnp.where(has_after, rows + 2 * psf_rim, rows + psf_rim)
    inside = (index >= low_edge) & (index < high_edge)

    def model_block(block, squares):
        start = pl.multiple_of(block * LANES, LANES)
        window = pl.ds(start, 2 * LANES)
        parts = []
        for step in range(steps):
            if step % 2 == 0:
                parts.append(ext[pl.ds(8 * step, model_rows), window])
            else:
                parts.append(ext_low[pl.ds(8 * (step - 1), model_rows), window])
        product = jnp.dot(
            jnp.concatenate(parts, axis=1), weights[...], preferred_element_type=f32
        )
        for s in range(8):
            y_model[s] = product[:, s * LANES : (s + 1) * LANES]
        first = EDGE - rim - psf_rim
        model = y_model[0, pl.ds(first, wide_rows), :]
        for s in range(1, 8):
            model = model + y_model[s, pl.ds(first + s, wide_rows), :]
        diff = sci_ext[pl.ds(8 - psf_rim, wide_rows), pl.ds(start, LANES)] - model
        diff = jnp.where(inside, diff, 0.0)
        diff_ext[:, pl.ds(start, LANES)] = diff
        own = diff[psf_rim : psf_rim + rows]
        difference_ref[:, pl.ds(start, LANES)] = own
        return squares + jnp.sum((own * own).reshape(rows // 8, 8, LANES), axis=0)

    partial[...] = lax.fori_loop(0, blocks, model_block, jnp.zeros((8, LANES), f32))
    part_copies = []
    for step in range(1, PIECES):
        part_copies.append(
            remote(partial, partials.at[pos], part_send.at[step - 1], part_recv.at[pos], peer(step))
        )
    for copy in part_copies:
        copy.start()
    partials[pos] = partial[...]

    tail = jnp.zeros((wide_rows, LANES), f32)
    diff_low[...] = pltpu.roll(jnp.concatenate([diff_ext[...], tail], axis=1), psf_rim, 1).astype(bf16)

    def psf_block(block, carry):
        start = pl.multiple_of(block * LANES, LANES)
        product = jnp.dot(
            diff_low[:, pl.ds(start, 2 * LANES)], psf_weights[...], preferred_element_type=f32
        )
        for s in range(psf_taps):
            y_psf[s] = product[:, s * LANES : (s + 1) * LANES]
        response = y_psf[0, pl.ds(0, rows), :]
        for s in range(1, psf_taps):
            response = response + y_psf[s, pl.ds(s, rows), :]
        detection_ref[:, pl.ds(start, LANES)] = response
        return carry

    lax.fori_loop(0, blocks, psf_block, 0)

    for step in range(1, PIECES):
        source = lax.rem(pos + step, PIECES)
        remote(
            partial, partials.at[source], part_send.at[step - 1], part_recv.at[source], peer(step)
        ).wait_recv()
    variance = jnp.sum(jnp.sum(partials[...], axis=0), keepdims=True) / (PIECES * rows * cols)
    detection_ref[...] = detection_ref[...] / jnp.sqrt(variance + 1e-06)

    pl.when(has_high)(to_high.wait_send)
    pl.when(has_low)(to_low.wait_send)
    pl.when(has_far)(to_far.wait_send)
    to_sibling.wait_send()
    pl.when(has_low)(from_low.wait_send)
    pl.when(has_high)(from_high.wait_send)
    pl.when(has_before)(sci_up.wait_send)
    pl.when(has_after)(sci_down.wait_send)
    pl.when(has_before)(halo_up.wait_send)
    pl.when(has_after)(halo_down.wait_send)
    for copy in part_copies:
        copy.wait_send()


def shards(
    science,
    template,
    owner_map,
    covering,
    row_shift,
    col_shift,
    basis_cols,
    basis_rows,
    coeffs,
    psf_kernel,
):
    rows, cols = science.shape
    devices = lax.axis_size("visit")
    steps = (basis_cols.shape[1] + 7) // 8
    psf_taps = psf_kernel.shape[0]
    f32, bf16 = jnp.float32, jnp.bfloat16
    smem = pl.BlockSpec(memory_space=pltpu.SMEM)
    vmem = pl.BlockSpec(memory_space=pltpu.VMEM)
    wide = cols + LANES
    dma = pltpu.SemaphoreType.DMA
    flops = 2 * cols * (rows + 32) * (2 * LANES) * (8 * steps + psf_taps)
    return pl.pallas_call(
        functools.partial(kernel, devices),
        out_shape=[jax.ShapeDtypeStruct((rows, cols), f32)] * 2,
        in_specs=[smem] * 4 + [vmem] * 6,
        out_specs=[vmem] * 2,
        scratch_shapes=[
            pltpu.VMEM((2 * REACH + 1, rows, cols), bf16),
            pltpu.VMEM((rows + 3 * EDGE, wide), bf16),
            pltpu.VMEM((rows + 2 * EDGE, wide), bf16),
            pltpu.VMEM((rows + 24, cols), f32),
            pltpu.VMEM((4, LANES, LANES), f32),
            pltpu.VMEM((2, LANES, 2 * LANES), f32),
            pltpu.VMEM((steps * 2 * LANES, 8 * LANES), bf16),
            pltpu.VMEM((2 * LANES, psf_taps * LANES), bf16),
            pltpu.VMEM((8, rows + 2 * EDGE, LANES), f32),
            pltpu.VMEM((psf_taps, rows + EDGE, LANES), f32),
            pltpu.VMEM((rows + EDGE, cols), f32),
            pltpu.VMEM((rows + EDGE, wide), bf16),
            pltpu.VMEM((8, LANES), f32),
            pltpu.VMEM((PIECES, 8, LANES), f32),
            dma((4,)),
            dma((2 * REACH + 1,)),
            dma((2,)),
            dma((2,)),
            dma((2,)),
            dma((2,)),
            dma((2,)),
            dma((PIECES - 1,)),
            dma((PIECES,)),
        ],
        compiler_params=pltpu.CompilerParams(
            collective_id=0, has_side_effects=True, vmem_limit_bytes=48 * 1024 * 1024
        ),
        cost_estimate=pl.CostEstimate(
            flops=flops, bytes_accessed=rows * cols * 14, transcendentals=0
        ),
    )(
        owner_map,
        covering,
        row_shift,
        col_shift,
        science,
        template,
        basis_cols,
        basis_rows,
        coeffs,
        psf_kernel,
    )


def solution(mesh):
    return jax.shard_map(
        shards,
        mesh=mesh,
        in_specs=(
            P(("groups", "visit"), None),
            P(("groups", "visit"), None),
            P("groups"),
            P(("groups", "visit"), None),
            P(("groups", "visit"), None),
            P(("groups", "visit"), None),
            P(),
            P(),
            P("groups", None),
            P(),
        ),
        out_specs=(P(("groups", "visit"), None), P(("groups", "visit"), None)),
        check_vma=False,
    )
```

```python
import functools

import jax
import jax.numpy as jnp
from jax import lax
from jax.experimental import pallas as pl
from jax.experimental.pallas import tpu as pltpu
from jax.sharding import PartitionSpec as P

PIECES = 4
REACH = 3
LANES = 128
EDGE = 16
MESH = pl.DeviceIdType.MESH


def kernel(
    devices,
    owner_hbm,
    covering_hbm,
    row_shift_hbm,
    col_shift_hbm,
    science_ref,
    template_ref,
    basis_cols_hbm,
    basis_rows_hbm,
    coeffs_hbm,
    psf_hbm,
    difference_ref,
    detection_ref,
    owner_ref,
    covering_ref,
    row_shift_ref,
    col_shift_ref,
    basis_cols_ref,
    basis_rows_ref,
    coeffs_ref,
    psf_ref,
    own_piece,
    slots_0,
    slots_1,
    slots_2,
    slots_3,
    moved,
    ext,
    ext_low,
    sci_ext,
    small,
    folded,
    weights,
    psf_weights,
    y_model,
    y_psf,
    diff_ext,
    diff_low,
    partial,
    partials,
    fetch,
    piece_send,
    piece_recv,
    relay_send,
    forward_send,
    sci_send,
    sci_recv,
    halo_send,
    halo_recv,
    part_send,
    part_recv,
):
    rows, cols = science_ref.shape
    blocks = cols // LANES
    taps = basis_cols_ref.shape[1]
    basis = basis_cols_ref.shape[0]
    psf_taps = psf_ref.shape[0]
    rim, psf_rim = taps // 2, psf_taps // 2
    f32, bf16 = jnp.float32, jnp.bfloat16

    group = lax.axis_index("groups")
    me = lax.axis_index("visit")
    core = lax.rem(me, 2)
    odd = lax.rem(me // 2, 2)
    sibling = me + 1 - 2 * core
    beside = me + 2 - 4 * odd
    onward = me + 4 - 8 * odd
    held = lax.rem(me + 1, devices)
    visit = held // PIECES
    pos = lax.rem(held, PIECES)
    before = lax.rem(me + devices - 1, devices)
    after = lax.rem(me + 1, devices)
    far = jnp.where(core == 1, me + REACH, me - REACH)
    has_onward = (onward >= 0) & (onward < devices)
    back = me - 4 + 8 * odd
    has_back = (back >= 0) & (back < devices)
    has_far = (far >= 0) & (far < devices)
    has_before, has_after = pos > 0, pos < PIECES - 1

    def peer(step):
        return lax.rem(visit * PIECES + lax.rem(pos + step, PIECES) + devices - 1, devices)

    barrier = pltpu.get_barrier_semaphore()

    def greet(device):
        pl.semaphore_signal(barrier, inc=1, device_id=(group, device), device_id_type=MESH)

    greet(sibling)
    greet(beside)
    for step in range(1, PIECES):
        greet(peer(step))
    pl.when(has_onward)(lambda: greet(onward))
    pl.when(has_back)(lambda: greet(back))
    pl.when(has_far)(lambda: greet(far))
    fetches = [
        pltpu.make_async_copy(src, dst, fetch.at[number])
        for number, (src, dst) in enumerate(
            (
                (owner_hbm, owner_ref),
                (covering_hbm, covering_ref),
                (row_shift_hbm, row_shift_ref),
                (col_shift_hbm, col_shift_ref),
                (basis_cols_hbm, basis_cols_ref),
                (basis_rows_hbm, basis_rows_ref),
                (coeffs_hbm, coeffs_ref),
                (psf_hbm, psf_ref),
                (template_ref, own_piece),
                (science_ref, sci_ext.at[pl.ds(8, rows)]),
            )
        )
    ]
    for copy in fetches:
        copy.start()
    expected = (
        PIECES
        + 1
        + has_onward.astype(jnp.int32)
        + has_back.astype(jnp.int32)
        + has_far.astype(jnp.int32)
    )
    pl.semaphore_wait(barrier, expected)

    def remote(src, dst, send, recv, device):
        return pltpu.make_async_remote_copy(
            src_ref=src,
            dst_ref=dst,
            send_sem=send,
            recv_sem=recv,
            device_id=(group, device),
            device_id_type=MESH,
        )

    slots = (slots_0, slots_1, slots_2, slots_3)
    chunks = len(slots)
    chunk_cols = cols // chunks

    def piece_copy(src, slot, chunk, send, device):
        return remote(src, slots[chunk].at[slot], send, piece_recv.at[slot, chunk], device)

    def own_chunk(chunk):
        return template_ref.at[:, pl.ds(chunk * chunk_cols, chunk_cols)]

    def arrival(slot, chunk):
        return piece_copy(slots[chunk].at[slot], slot, chunk, piece_send.at[0, chunk], sibling)

    beside_slot = 5 - 4 * odd
    back_slot = 1 + 4 * odd
    far_slot = jnp.where(core == 1, 0, 2 * REACH)
    to_beside, to_far, to_sibling, to_onward, from_beside, from_back = [], [], [], [], [], []
    for chunk in range(chunks):
        src = own_chunk(chunk)
        to_beside.append(piece_copy(src, back_slot, chunk, piece_send.at[0, chunk], beside))
        to_far.append(piece_copy(src, far_slot, chunk, piece_send.at[1, chunk], far))
        to_sibling.append(piece_copy(src, 2 + 2 * core, chunk, piece_send.at[2, chunk], sibling))
        beside_chunk, back_chunk = slots[chunk].at[beside_slot], slots[chunk].at[back_slot]
        to_onward.append(piece_copy(beside_chunk, back_slot, chunk, relay_send.at[chunk], onward))
        from_beside.append(
            piece_copy(beside_chunk, beside_slot - 1 + 2 * core, chunk, forward_send.at[0, chunk], sibling)
        )
        from_back.append(
            piece_copy(back_chunk, back_slot - 1 + 2 * core, chunk, forward_send.at[1, chunk], sibling)
        )
    sci_up = remote(
        science_ref.at[pl.ds(0, 8)], sci_ext.at[pl.ds(8 + rows, 8)], sci_send.at[0], sci_recv.at[1], before
    )
    sci_down = remote(
        science_ref.at[pl.ds(rows - 8, 8)], sci_ext.at[pl.ds(0, 8)], sci_send.at[1], sci_recv.at[0], after
    )
    for chunk in range(chunks):
        to_beside[chunk].start()
        pl.when(has_far)(to_far[chunk].start)
        to_sibling[chunk].start()
    pl.when(has_before)(sci_up.start)
    pl.when(has_after)(sci_down.start)
    for copy in fetches:
        copy.wait()

    lane = lax.broadcasted_iota(jnp.int32, (LANES, 2 * LANES), 1)
    tap = lax.broadcasted_iota(jnp.int32, (LANES, 2 * LANES), 0)
    reverse = jnp.where(lax.rem(tap + lane, 2 * LANES) == 0, 1.0, 0.0).astype(bf16)
    small[...] = jnp.zeros_like(small)
    small[0, 0:basis, 0:taps] = basis_cols_ref[...]
    small[1, 0:basis, 0:taps] = basis_rows_ref[...]
    small[2, 0:psf_taps, 0:psf_taps] = psf_ref[...]
    small[3, 0:1, 0:basis] = coeffs_ref[pl.ds(visit, 1), :]
    diagonal = lax.broadcasted_iota(jnp.int32, (LANES, LANES), 0) == lax.broadcasted_iota(
        jnp.int32, (LANES, LANES), 1
    )
    coeff_col = jnp.sum(
        jnp.where(diagonal, jnp.broadcast_to(small[3, 0:1, :], (LANES, LANES)), 0.0),
        axis=1,
        keepdims=True,
    )
    row_weights = (coeff_col * small[1]).astype(bf16).astype(f32)
    cols_reversed = jnp.dot(small[0].astype(bf16), reverse, preferred_element_type=f32)
    folded[0] = jnp.dot(
        row_weights.T.astype(bf16), cols_reversed.astype(bf16), preferred_element_type=f32
    )
    folded[1] = jnp.dot(small[2].astype(bf16), reverse, preferred_element_type=f32)

    def band(which, index):
        line = folded[which, pl.ds(index, 1), :]
        spread = jnp.broadcast_to(line, (2 * LANES, 2 * LANES))
        rolled = pltpu.roll(spread, 0, 1, stride=1, stride_axis=0)
        return rolled[:, :LANES].astype(bf16)

    steps = (taps + 7) // 8

    def build(step, carry):
        start = pl.multiple_of(step * (2 * LANES), 2 * LANES)
        for s in range(8):
            weights[pl.ds(start, 2 * LANES), s * LANES : (s + 1) * LANES] = band(0, step * 8 + s)
        return carry

    lax.fori_loop(0, steps, build, 0)
    for s in range(psf_taps):
        psf_weights[:, s * LANES : (s + 1) * LANES] = band(1, s)

    sci_ext[pl.ds(rows + 16, 8), :] = jnp.zeros((8, cols), f32)
    ext[pl.ds(rows + 2 * EDGE, EDGE), :] = jnp.zeros((EDGE, ext.shape[1]), bf16)
    pad_blocks = (moved.shape[1] - blocks) // 2
    margin = pad_blocks * LANES
    for part in range(pad_blocks):
        for k in range(moved.shape[0]):
            moved[k, part] = jnp.zeros((rows, LANES), f32)
            moved[k, pad_blocks + blocks + part] = jnp.zeros((rows, LANES), f32)
    for part in range(blocks):
        moved[0, pad_blocks + part] = own_piece[:, part * LANES : (part + 1) * LANES].astype(f32)

    @pl.when(jnp.logical_not(has_before))
    def _():
        sci_ext[pl.ds(0, 8), :] = jnp.zeros((8, cols), f32)
        ext[pl.ds(0, EDGE), :] = jnp.zeros((EDGE, ext.shape[1]), bf16)

    @pl.when(jnp.logical_not(has_after))
    def _():
        sci_ext[pl.ds(rows + 8, 8), :] = jnp.zeros((8, cols), f32)
        ext[pl.ds(rows + EDGE, EDGE), :] = jnp.zeros((EDGE, ext.shape[1]), bf16)

    slot_count = moved.shape[0]
    row_to = lax.broadcasted_iota(jnp.int32, (rows, rows), 0)
    row_from = lax.broadcasted_iota(jnp.int32, (rows, rows), 1)
    places, row_offs, col_offs, selects = [None], [None], [0], [None]
    for k in range(1, slot_count):
        holder = owner_ref[covering_ref[0, k]]
        places.append(jnp.clip(holder - me + REACH, 0, 2 * REACH))
        row_offs.append(row_shift_ref[0, k])
        col_offs.append(col_shift_ref[0, k])
        selects.append(jnp.where(row_to - row_from == row_offs[k], 1.0, 0.0).astype(bf16))

    def pass_on(chunk):
        arrival(beside_slot, chunk).wait_recv()
        pl.when(has_onward)(to_onward[chunk].start)
        from_beside[chunk].start()

    def canvas_block(start, width):
        col = lax.broadcasted_iota(jnp.int32, (1, width), 1) + (start - rim)
        row = lax.broadcasted_iota(jnp.int32, (rows, width), 0)
        total, coverage = None, jnp.ones((rows, width), f32)
        for k in range(slot_count):
            first = margin + start - rim - col_offs[k]
            base = first // LANES if k == 0 else lax.div(first, LANES)
            span = width // LANES + 1
            window = jnp.concatenate([moved[k, base + part] for part in range(span)], axis=1)
            turn = lax.rem(span * LANES - (first - base * LANES), span * LANES)
            placed = pltpu.roll(window, turn, 1)[:, :width]
            total = placed if k == 0 else total + placed
            if k:
                col_old, row_old = col - col_offs[k], row - row_offs[k]
                col_in = jnp.where((col_old >= 0) & (col_old < cols), 1.0, 0.0)
                row_in = jnp.where((row_old >= 0) & (row_old < rows), 1.0, 0.0)
                coverage = coverage + row_in * col_in
        image = jnp.where((col >= 0) & (col < cols), total / coverage, 0.0)
        ext[pl.ds(EDGE, rows), start : start + width] = image.astype(bf16)

    pass_on(0)
    for chunk in range(chunks):
        if chunk + 1 < chunks:
            pass_on(chunk + 1)

        @pl.when(has_back)
        def _():
            arrival(back_slot, chunk).wait_recv()
            from_back[chunk].start()

        for slot in (0, 2, 4, 6):
            origin = me + slot - REACH
            pl.when((origin >= 0) & (origin < devices))(arrival(slot, chunk).wait_recv)
        for k in range(1, slot_count):
            product = jnp.dot(selects[k], slots[chunk][places[k]], preferred_element_type=f32)
            for part in range(chunk_cols // LANES):
                moved[k, pad_blocks + chunk * (chunk_cols // LANES) + part] = product[
                    :, part * LANES : (part + 1) * LANES
                ]
        if chunk:
            canvas_block((chunk - 1) * chunk_cols, chunk_cols)
    canvas_block(cols - chunk_cols, chunk_cols)
    canvas_block(cols, LANES)

    halo_up = remote(
        ext.at[pl.ds(EDGE, EDGE)], ext.at[pl.ds(rows + EDGE, EDGE)], halo_send.at[0], halo_recv.at[1], before
    )
    halo_down = remote(
        ext.at[pl.ds(rows, EDGE)], ext.at[pl.ds(0, EDGE)], halo_send.at[1], halo_recv.at[0], after
    )
    pl.when(has_before)(halo_up.start)
    pl.when(has_after)(halo_down.start)

    @pl.when(has_before)
    def _():
        halo_down.wait_recv()
        sci_down.wait_recv()

    @pl.when(has_after)
    def _():
        halo_up.wait_recv()
        sci_up.wait_recv()

    ext_low[...] = ext[...].astype(f32)[8 : rows + 2 * EDGE + 8].astype(bf16)
    model_rows = rows + 2 * EDGE
    wide_rows = rows + EDGE
    index = lax.broadcasted_iota(jnp.int32, (wide_rows, LANES), 0)
    low_edge = jnp.where(has_before, 0, psf_rim)
    high_edge = jnp.where(has_after, rows + 2 * psf_rim, rows + psf_rim)
    inside = (index >= low_edge) & (index < high_edge)

    def model_block(block, squares):
        start = pl.multiple_of(block * LANES, LANES)
        window = pl.ds(start, 2 * LANES)
        parts = []
        for step in range(steps):
            if step % 2 == 0:
                parts.append(ext[pl.ds(8 * step, model_rows), window])
            else:
                parts.append(ext_low[pl.ds(8 * (step - 1), model_rows), window])
        product = jnp.dot(
            jnp.concatenate(parts, axis=1), weights[...], preferred_element_type=f32
        )
        for s in range(8):
            y_model[s] = product[:, s * LANES : (s + 1) * LANES]
        first = EDGE - rim - psf_rim
        model = y_model[0, pl.ds(first, wide_rows), :]
        for s in range(1, 8):
            model = model + y_model[s, pl.ds(first + s, wide_rows), :]
        diff = sci_ext[pl.ds(8 - psf_rim, wide_rows), pl.ds(start, LANES)] - model
        diff = jnp.where(inside, diff, 0.0)
        diff_ext[:, pl.ds(start, LANES)] = diff
        own = diff[psf_rim : psf_rim + rows]
        difference_ref[:, pl.ds(start, LANES)] = own
        return squares + jnp.sum((own * own).reshape(rows // 8, 8, LANES), axis=0)

    partial[...] = lax.fori_loop(0, blocks, model_block, jnp.zeros((8, LANES), f32))
    part_copies = []
    for step in range(1, PIECES):
        part_copies.append(
            remote(partial, partials.at[pos], part_send.at[step - 1], part_recv.at[pos], peer(step))
        )
    for copy in part_copies:
        copy.start()
    partials[pos] = partial[...]

    tail = jnp.zeros((wide_rows, LANES), f32)
    diff_low[...] = pltpu.roll(jnp.concatenate([diff_ext[...], tail], axis=1), psf_rim, 1).astype(bf16)

    def psf_block(block, carry):
        start = pl.multiple_of(block * LANES, LANES)
        product = jnp.dot(
            diff_low[:, pl.ds(start, 2 * LANES)], psf_weights[...], preferred_element_type=f32
        )
        for s in range(psf_taps):
            y_psf[s] = product[:, s * LANES : (s + 1) * LANES]
        response = y_psf[0, pl.ds(0, rows), :]
        for s in range(1, psf_taps):
            response = response + y_psf[s, pl.ds(s, rows), :]
        detection_ref[:, pl.ds(start, LANES)] = response
        return carry

    lax.fori_loop(0, blocks, psf_block, 0)

    for step in range(1, PIECES):
        source = lax.rem(pos + step, PIECES)
        remote(
            partial, partials.at[source], part_send.at[step - 1], part_recv.at[source], peer(step)
        ).wait_recv()
    variance = jnp.sum(jnp.sum(partials[...], axis=0), keepdims=True) / (PIECES * rows * cols)
    detection_ref[...] = detection_ref[...] / jnp.sqrt(variance + 1e-06)

    for chunk in range(chunks):
        to_beside[chunk].wait_send()
        pl.when(has_far)(to_far[chunk].wait_send)
        to_sibling[chunk].wait_send()
        pl.when(has_onward)(to_onward[chunk].wait_send)
        from_beside[chunk].wait_send()
        pl.when(has_back)(from_back[chunk].wait_send)
    pl.when(has_before)(sci_up.wait_send)
    pl.when(has_after)(sci_down.wait_send)
    pl.when(has_before)(halo_up.wait_send)
    pl.when(has_after)(halo_down.wait_send)
    for copy in part_copies:
        copy.wait_send()


def shards(
    science,
    template,
    owner_map,
    covering,
    row_shift,
    col_shift,
    basis_cols,
    basis_rows,
    coeffs,
    psf_kernel,
):
    rows, cols = science.shape
    devices = lax.axis_size("visit")
    steps = (basis_cols.shape[1] + 7) // 8
    psf_taps = psf_kernel.shape[0]
    f32, bf16 = jnp.float32, jnp.bfloat16
    hbm = pl.BlockSpec(memory_space=pl.ANY)
    chunks = 4
    slot_count = covering.shape[1]
    vmem = pl.BlockSpec(memory_space=pltpu.VMEM)
    wide = cols + LANES
    dma = pltpu.SemaphoreType.DMA
    flops = 2 * cols * (rows + 32) * (2 * LANES) * (8 * steps + psf_taps)
    return pl.pallas_call(
        functools.partial(kernel, devices),
        out_shape=[jax.ShapeDtypeStruct((rows, cols), f32)] * 2,
        in_specs=[hbm] * 10,
        out_specs=[vmem] * 2,
        scratch_shapes=[
            pltpu.SMEM(owner_map.shape, jnp.int32),
            pltpu.SMEM(covering.shape, jnp.int32),
            pltpu.SMEM(row_shift.shape, jnp.int32),
            pltpu.SMEM(col_shift.shape, jnp.int32),
            pltpu.VMEM(basis_cols.shape, f32),
            pltpu.VMEM(basis_rows.shape, f32),
            pltpu.VMEM(coeffs.shape, f32),
            pltpu.VMEM(psf_kernel.shape, f32),
            pltpu.VMEM((rows, cols), bf16),
            *([pltpu.VMEM((2 * REACH + 1, rows, cols // chunks), bf16)] * chunks),
            pltpu.VMEM((slot_count, cols // LANES + 6, rows, LANES), f32),
            pltpu.VMEM((rows + 3 * EDGE, wide), bf16),
            pltpu.VMEM((rows + 2 * EDGE, wide), bf16),
            pltpu.VMEM((rows + 24, cols), f32),
            pltpu.VMEM((4, LANES, LANES), f32),
            pltpu.VMEM((2, LANES, 2 * LANES), f32),
            pltpu.VMEM((steps * 2 * LANES, 8 * LANES), bf16),
            pltpu.VMEM((2 * LANES, psf_taps * LANES), bf16),
            pltpu.VMEM((8, rows + 2 * EDGE, LANES), f32),
            pltpu.VMEM((psf_taps, rows + EDGE, LANES), f32),
            pltpu.VMEM((rows + EDGE, cols), f32),
            pltpu.VMEM((rows + EDGE, wide), bf16),
            pltpu.VMEM((8, LANES), f32),
            pltpu.VMEM((PIECES, 8, LANES), f32),
            dma((10,)),
            dma((3, chunks)),
            dma((2 * REACH + 1, chunks)),
            dma((chunks,)),
            dma((2, chunks)),
            dma((2,)),
            dma((2,)),
            dma((2,)),
            dma((2,)),
            dma((PIECES - 1,)),
            dma((PIECES,)),
        ],
        compiler_params=pltpu.CompilerParams(
            collective_id=0, has_side_effects=True, vmem_limit_bytes=60 * 1024 * 1024
        ),
        cost_estimate=pl.CostEstimate(
            flops=flops, bytes_accessed=rows * cols * 14, transcendentals=0
        ),
    )(
        owner_map,
        covering,
        row_shift,
        col_shift,
        science,
        template,
        basis_cols,
        basis_rows,
        coeffs,
        psf_kernel,
    )


def solution(mesh):
    return jax.shard_map(
        shards,
        mesh=mesh,
        in_specs=(
            P(("groups", "visit"), None),
            P(("groups", "visit"), None),
            P("groups"),
            P(("groups", "visit"), None),
            P(("groups", "visit"), None),
            P(("groups", "visit"), None),
            P(),
            P(),
            P("groups", None),
            P(),
        ),
        out_specs=(P(("groups", "visit"), None), P(("groups", "visit"), None)),
        check_vma=False,
    )
```

```python
import functools

import jax
import jax.numpy as jnp
from jax import lax
from jax.experimental import pallas as pl
from jax.experimental.pallas import tpu as pltpu
from jax.sharding import PartitionSpec as P

PIECES = 4
REACH = 3
LANES = 128
EDGE = 16
MESH = pl.DeviceIdType.MESH


def kernel(
    devices,
    owner_hbm,
    covering_hbm,
    row_shift_hbm,
    col_shift_hbm,
    science_ref,
    template_ref,
    basis_cols_hbm,
    basis_rows_hbm,
    coeffs_hbm,
    psf_hbm,
    difference_ref,
    detection_ref,
    owner_ref,
    covering_ref,
    row_shift_ref,
    col_shift_ref,
    basis_cols_ref,
    basis_rows_ref,
    coeffs_ref,
    psf_ref,
    own_piece,
    slots_0,
    slots_1,
    slots_2,
    slots_3,
    slots_4,
    slots_5,
    slots_6,
    slots_7,
    moved,
    ext,
    ext_low,
    sci_ext,
    small,
    folded,
    weights,
    psf_weights,
    y_model,
    y_psf,
    diff_ext,
    diff_low,
    partial,
    partials,
    fetch,
    piece_send,
    piece_recv,
    relay_send,
    forward_send,
    sci_send,
    sci_recv,
    halo_send,
    halo_recv,
    part_send,
    part_recv,
):
    rows, cols = science_ref.shape
    blocks = cols // LANES
    taps = basis_cols_ref.shape[1]
    basis = basis_cols_ref.shape[0]
    psf_taps = psf_ref.shape[0]
    rim, psf_rim = taps // 2, psf_taps // 2
    f32, bf16 = jnp.float32, jnp.bfloat16

    group = lax.axis_index("groups")
    me = lax.axis_index("visit")
    core = lax.rem(me, 2)
    odd = lax.rem(me // 2, 2)
    sibling = me + 1 - 2 * core
    beside = me + 2 - 4 * odd
    onward = me + 4 - 8 * odd
    held = lax.rem(me + 1, devices)
    visit = held // PIECES
    pos = lax.rem(held, PIECES)
    before = lax.rem(me + devices - 1, devices)
    after = lax.rem(me + 1, devices)
    far = jnp.where(core == 1, me + REACH, me - REACH)
    has_onward = (onward >= 0) & (onward < devices)
    back = me - 4 + 8 * odd
    has_back = (back >= 0) & (back < devices)
    has_far = (far >= 0) & (far < devices)
    has_before, has_after = pos > 0, pos < PIECES - 1

    def peer(step):
        return lax.rem(visit * PIECES + lax.rem(pos + step, PIECES) + devices - 1, devices)

    barrier = pltpu.get_barrier_semaphore()

    def greet(device):
        pl.semaphore_signal(barrier, inc=1, device_id=(group, device), device_id_type=MESH)

    greet(sibling)
    greet(beside)
    for step in range(1, PIECES):
        greet(peer(step))
    pl.when(has_onward)(lambda: greet(onward))
    pl.when(has_back)(lambda: greet(back))
    pl.when(has_far)(lambda: greet(far))
    fetches = [
        pltpu.make_async_copy(src, dst, fetch.at[number])
        for number, (src, dst) in enumerate(
            (
                (owner_hbm, owner_ref),
                (covering_hbm, covering_ref),
                (row_shift_hbm, row_shift_ref),
                (col_shift_hbm, col_shift_ref),
                (basis_cols_hbm, basis_cols_ref),
                (basis_rows_hbm, basis_rows_ref),
                (coeffs_hbm, coeffs_ref),
                (psf_hbm, psf_ref),
                (template_ref, own_piece),
                (science_ref, sci_ext.at[pl.ds(8, rows)]),
            )
        )
    ]
    for copy in fetches:
        copy.start()
    expected = (
        PIECES
        + 1
        + has_onward.astype(jnp.int32)
        + has_back.astype(jnp.int32)
        + has_far.astype(jnp.int32)
    )
    pl.semaphore_wait(barrier, expected)

    def remote(src, dst, send, recv, device):
        return pltpu.make_async_remote_copy(
            src_ref=src,
            dst_ref=dst,
            send_sem=send,
            recv_sem=recv,
            device_id=(group, device),
            device_id_type=MESH,
        )

    slots = (slots_0, slots_1, slots_2, slots_3, slots_4, slots_5, slots_6, slots_7)
    chunks = len(slots)
    chunk_cols = cols // chunks

    def piece_copy(src, slot, chunk, send, device):
        return remote(src, slots[chunk].at[slot], send, piece_recv.at[slot, chunk], device)

    def own_chunk(chunk):
        return template_ref.at[:, pl.ds(chunk * chunk_cols, chunk_cols)]

    def arrival(slot, chunk):
        return piece_copy(slots[chunk].at[slot], slot, chunk, piece_send.at[0, chunk], sibling)

    beside_slot = 5 - 4 * odd
    back_slot = 1 + 4 * odd
    far_slot = jnp.where(core == 1, 0, 2 * REACH)
    to_beside, to_far, to_sibling, to_onward, from_beside, from_back = [], [], [], [], [], []
    for chunk in range(chunks):
        src = own_chunk(chunk)
        to_beside.append(piece_copy(src, back_slot, chunk, piece_send.at[0, chunk], beside))
        to_far.append(piece_copy(src, far_slot, chunk, piece_send.at[1, chunk], far))
        to_sibling.append(piece_copy(src, 2 + 2 * core, chunk, piece_send.at[2, chunk], sibling))
        beside_chunk, back_chunk = slots[chunk].at[beside_slot], slots[chunk].at[back_slot]
        to_onward.append(piece_copy(beside_chunk, back_slot, chunk, relay_send.at[chunk], onward))
        from_beside.append(
            piece_copy(beside_chunk, beside_slot - 1 + 2 * core, chunk, forward_send.at[0, chunk], sibling)
        )
        from_back.append(
            piece_copy(back_chunk, back_slot - 1 + 2 * core, chunk, forward_send.at[1, chunk], sibling)
        )
    sci_up = remote(
        science_ref.at[pl.ds(0, 8)], sci_ext.at[pl.ds(8 + rows, 8)], sci_send.at[0], sci_recv.at[1], before
    )
    sci_down = remote(
        science_ref.at[pl.ds(rows - 8, 8)], sci_ext.at[pl.ds(0, 8)], sci_send.at[1], sci_recv.at[0], after
    )
    for chunk in range(chunks):
        to_beside[chunk].start()
        pl.when(has_far)(to_far[chunk].start)
        to_sibling[chunk].start()
    pl.when(has_before)(sci_up.start)
    pl.when(has_after)(sci_down.start)
    for copy in fetches:
        copy.wait()

    lane = lax.broadcasted_iota(jnp.int32, (LANES, 2 * LANES), 1)
    tap = lax.broadcasted_iota(jnp.int32, (LANES, 2 * LANES), 0)
    reverse = jnp.where(lax.rem(tap + lane, 2 * LANES) == 0, 1.0, 0.0).astype(bf16)
    small[...] = jnp.zeros_like(small)
    small[0, 0:basis, 0:taps] = basis_cols_ref[...]
    small[1, 0:basis, 0:taps] = basis_rows_ref[...]
    small[2, 0:psf_taps, 0:psf_taps] = psf_ref[...]
    small[3, 0:1, 0:basis] = coeffs_ref[pl.ds(visit, 1), :]
    diagonal = lax.broadcasted_iota(jnp.int32, (LANES, LANES), 0) == lax.broadcasted_iota(
        jnp.int32, (LANES, LANES), 1
    )
    coeff_col = jnp.sum(
        jnp.where(diagonal, jnp.broadcast_to(small[3, 0:1, :], (LANES, LANES)), 0.0),
        axis=1,
        keepdims=True,
    )
    row_weights = (coeff_col * small[1]).astype(bf16).astype(f32)
    cols_reversed = jnp.dot(small[0].astype(bf16), reverse, preferred_element_type=f32)
    folded[0] = jnp.dot(
        row_weights.T.astype(bf16), cols_reversed.astype(bf16), preferred_element_type=f32
    )
    folded[1] = jnp.dot(small[2].astype(bf16), reverse, preferred_element_type=f32)

    def band(which, index):
        line = folded[which, pl.ds(index, 1), :]
        spread = jnp.broadcast_to(line, (2 * LANES, 2 * LANES))
        rolled = pltpu.roll(spread, 0, 1, stride=1, stride_axis=0)
        return rolled[:, :LANES].astype(bf16)

    steps = (taps + 7) // 8

    def build(step, carry):
        start = pl.multiple_of(step * (2 * LANES), 2 * LANES)
        for s in range(8):
            weights[pl.ds(start, 2 * LANES), s * LANES : (s + 1) * LANES] = band(0, step * 8 + s)
        return carry

    lax.fori_loop(0, steps, build, 0)
    for s in range(psf_taps):
        psf_weights[:, s * LANES : (s + 1) * LANES] = band(1, s)

    sci_ext[pl.ds(rows + 16, 8), :] = jnp.zeros((8, cols), f32)
    ext[pl.ds(rows + 2 * EDGE, EDGE), :] = jnp.zeros((EDGE, ext.shape[1]), bf16)
    pad_blocks = (moved.shape[1] - blocks) // 2
    margin = pad_blocks * LANES
    for part in range(pad_blocks):
        for k in range(moved.shape[0]):
            moved[k, part] = jnp.zeros((rows, LANES), f32)
            moved[k, pad_blocks + blocks + part] = jnp.zeros((rows, LANES), f32)
    for part in range(blocks):
        moved[0, pad_blocks + part] = own_piece[:, part * LANES : (part + 1) * LANES].astype(f32)

    @pl.when(jnp.logical_not(has_before))
    def _():
        sci_ext[pl.ds(0, 8), :] = jnp.zeros((8, cols), f32)
        ext[pl.ds(0, EDGE), :] = jnp.zeros((EDGE, ext.shape[1]), bf16)

    @pl.when(jnp.logical_not(has_after))
    def _():
        sci_ext[pl.ds(rows + 8, 8), :] = jnp.zeros((8, cols), f32)
        ext[pl.ds(rows + EDGE, EDGE), :] = jnp.zeros((EDGE, ext.shape[1]), bf16)

    slot_count = moved.shape[0]
    row_to = lax.broadcasted_iota(jnp.int32, (rows, rows), 0)
    row_from = lax.broadcasted_iota(jnp.int32, (rows, rows), 1)
    places, row_offs, col_offs, selects = [None], [None], [0], [None]
    for k in range(1, slot_count):
        holder = owner_ref[covering_ref[0, k]]
        places.append(jnp.clip(holder - me + REACH, 0, 2 * REACH))
        row_offs.append(row_shift_ref[0, k])
        col_offs.append(col_shift_ref[0, k])
        selects.append(jnp.where(row_to - row_from == row_offs[k], 1.0, 0.0).astype(bf16))

    def pass_on(chunk):
        arrival(beside_slot, chunk).wait_recv()
        pl.when(has_onward)(to_onward[chunk].start)
        from_beside[chunk].start()

    def canvas_block(start, width):
        col = lax.broadcasted_iota(jnp.int32, (1, width), 1) + (start - rim)
        row = lax.broadcasted_iota(jnp.int32, (rows, width), 0)
        total, coverage = None, jnp.ones((rows, width), f32)
        for k in range(slot_count):
            first = margin + start - rim - col_offs[k]
            base = first // LANES if k == 0 else lax.div(first, LANES)
            span = width // LANES + 1
            window = jnp.concatenate([moved[k, base + part] for part in range(span)], axis=1)
            turn = lax.rem(span * LANES - (first - base * LANES), span * LANES)
            placed = pltpu.roll(window, turn, 1)[:, :width]
            total = placed if k == 0 else total + placed
            if k:
                col_old, row_old = col - col_offs[k], row - row_offs[k]
                col_in = jnp.where((col_old >= 0) & (col_old < cols), 1.0, 0.0)
                row_in = jnp.where((row_old >= 0) & (row_old < rows), 1.0, 0.0)
                coverage = coverage + row_in * col_in
        image = jnp.where((col >= 0) & (col < cols), total / coverage, 0.0)
        ext[pl.ds(EDGE, rows), start : start + width] = image.astype(bf16)

    def halo_copies(block):
        columns = pl.ds(block * LANES, LANES)
        up = remote(
            ext.at[pl.ds(EDGE, EDGE), columns],
            ext.at[pl.ds(rows + EDGE, EDGE), columns],
            halo_send.at[0, block],
            halo_recv.at[1, block],
            before,
        )
        down = remote(
            ext.at[pl.ds(rows, EDGE), columns],
            ext.at[pl.ds(0, EDGE), columns],
            halo_send.at[1, block],
            halo_recv.at[0, block],
            after,
        )
        return up, down

    halos = [halo_copies(block) for block in range(blocks + 1)]

    def canvas_and_halo(block):
        canvas_block(block * LANES, LANES)
        pl.when(has_before)(halos[block][0].start)
        pl.when(has_after)(halos[block][1].start)

    def finish_block(block):
        pl.when(has_before)(halos[block][1].wait_recv)
        pl.when(has_after)(halos[block][0].wait_recv)
        columns = slice(block * LANES, (block + 1) * LANES)
        ext_low[:, columns] = ext[:, columns].astype(f32)[8 : rows + 2 * EDGE + 8].astype(bf16)

    model_rows = rows + 2 * EDGE
    wide_rows = rows + EDGE
    index = lax.broadcasted_iota(jnp.int32, (wide_rows, LANES), 0)
    low_edge = jnp.where(has_before, 0, psf_rim)
    high_edge = jnp.where(has_after, rows + 2 * psf_rim, rows + psf_rim)
    inside = (index >= low_edge) & (index < high_edge)

    def model_block(block, squares):
        finish_block(block + 1)
        start = block * LANES
        window = pl.ds(start, 2 * LANES)
        parts = []
        for step in range(steps):
            if step % 2 == 0:
                parts.append(ext[pl.ds(8 * step, model_rows), window])
            else:
                parts.append(ext_low[pl.ds(8 * (step - 1), model_rows), window])
        product = jnp.dot(
            jnp.concatenate(parts, axis=1), weights[...], preferred_element_type=f32
        )
        for s in range(8):
            y_model[s] = product[:, s * LANES : (s + 1) * LANES]
        first = EDGE - rim - psf_rim
        model = y_model[0, pl.ds(first, wide_rows), :]
        for s in range(1, 8):
            model = model + y_model[s, pl.ds(first + s, wide_rows), :]
        diff = sci_ext[pl.ds(8 - psf_rim, wide_rows), pl.ds(start, LANES)] - model
        diff = jnp.where(inside, diff, 0.0)
        diff_ext[:, pl.ds(start, LANES)] = diff
        own = diff[psf_rim : psf_rim + rows]
        difference_ref[:, pl.ds(start, LANES)] = own
        return squares + jnp.sum((own * own).reshape(rows // 8, 8, LANES), axis=0)

    ahead = 2
    squares = jnp.zeros((8, LANES), f32)
    for chunk in range(ahead):
        pass_on(chunk)
    for chunk in range(chunks):
        if chunk + ahead < chunks:
            pass_on(chunk + ahead)

        @pl.when(has_back)
        def _():
            arrival(back_slot, chunk).wait_recv()
            from_back[chunk].start()

        for slot in (0, 2, 4, 6):
            origin = me + slot - REACH
            pl.when((origin >= 0) & (origin < devices))(arrival(slot, chunk).wait_recv)
        for k in range(1, slot_count):
            moved[k, pad_blocks + chunk] = jnp.dot(
                selects[k], slots[chunk][places[k]], preferred_element_type=f32
            )
        if chunk >= 2:
            canvas_and_halo(chunk - 2)
        if chunk == 3:
            pl.when(has_before)(sci_down.wait_recv)
            pl.when(has_after)(sci_up.wait_recv)
            finish_block(0)
        if chunk >= 4:
            squares = model_block(chunk - 4, squares)
    for block in range(blocks - 2, blocks + 1):
        canvas_and_halo(block)
    for block in range(blocks - 4, blocks):
        squares = model_block(block, squares)
    partial[...] = squares
    part_copies = []
    for step in range(1, PIECES):
        part_copies.append(
            remote(partial, partials.at[pos], part_send.at[step - 1], part_recv.at[pos], peer(step))
        )
    for copy in part_copies:
        copy.start()
    partials[pos] = partial[...]

    tail = jnp.zeros((wide_rows, LANES), f32)
    diff_low[...] = pltpu.roll(jnp.concatenate([diff_ext[...], tail], axis=1), psf_rim, 1).astype(bf16)

    def psf_block(block, carry):
        start = pl.multiple_of(block * LANES, LANES)
        product = jnp.dot(
            diff_low[:, pl.ds(start, 2 * LANES)], psf_weights[...], preferred_element_type=f32
        )
        for s in range(psf_taps):
            y_psf[s] = product[:, s * LANES : (s + 1) * LANES]
        response = y_psf[0, pl.ds(0, rows), :]
        for s in range(1, psf_taps):
            response = response + y_psf[s, pl.ds(s, rows), :]
        detection_ref[:, pl.ds(start, LANES)] = response
        return carry

    lax.fori_loop(0, blocks, psf_block, 0)

    for step in range(1, PIECES):
        source = lax.rem(pos + step, PIECES)
        remote(
            partial, partials.at[source], part_send.at[step - 1], part_recv.at[source], peer(step)
        ).wait_recv()
    variance = jnp.sum(jnp.sum(partials[...], axis=0), keepdims=True) / (PIECES * rows * cols)
    detection_ref[...] = detection_ref[...] / jnp.sqrt(variance + 1e-06)

    for chunk in range(chunks):
        to_beside[chunk].wait_send()
        pl.when(has_far)(to_far[chunk].wait_send)
        to_sibling[chunk].wait_send()
        pl.when(has_onward)(to_onward[chunk].wait_send)
        from_beside[chunk].wait_send()
        pl.when(has_back)(from_back[chunk].wait_send)
    pl.when(has_before)(sci_up.wait_send)
    pl.when(has_after)(sci_down.wait_send)
    for up, down in halos:
        pl.when(has_before)(up.wait_send)
        pl.when(has_after)(down.wait_send)
    for copy in part_copies:
        copy.wait_send()


def shards(
    science,
    template,
    owner_map,
    covering,
    row_shift,
    col_shift,
    basis_cols,
    basis_rows,
    coeffs,
    psf_kernel,
):
    rows, cols = science.shape
    devices = lax.axis_size("visit")
    steps = (basis_cols.shape[1] + 7) // 8
    psf_taps = psf_kernel.shape[0]
    f32, bf16 = jnp.float32, jnp.bfloat16
    hbm = pl.BlockSpec(memory_space=pl.ANY)
    chunks = 8
    slot_count = covering.shape[1]
    vmem = pl.BlockSpec(memory_space=pltpu.VMEM)
    wide = cols + LANES
    dma = pltpu.SemaphoreType.DMA
    flops = 2 * cols * (rows + 32) * (2 * LANES) * (8 * steps + psf_taps)
    return pl.pallas_call(
        functools.partial(kernel, devices),
        out_shape=[jax.ShapeDtypeStruct((rows, cols), f32)] * 2,
        in_specs=[hbm] * 10,
        out_specs=[vmem] * 2,
        scratch_shapes=[
            pltpu.SMEM(owner_map.shape, jnp.int32),
            pltpu.SMEM(covering.shape, jnp.int32),
            pltpu.SMEM(row_shift.shape, jnp.int32),
            pltpu.SMEM(col_shift.shape, jnp.int32),
            pltpu.VMEM(basis_cols.shape, f32),
            pltpu.VMEM(basis_rows.shape, f32),
            pltpu.VMEM(coeffs.shape, f32),
            pltpu.VMEM(psf_kernel.shape, f32),
            pltpu.VMEM((rows, cols), bf16),
            *([pltpu.VMEM((2 * REACH + 1, rows, cols // chunks), bf16)] * chunks),
            pltpu.VMEM((slot_count, cols // LANES + 6, rows, LANES), f32),
            pltpu.VMEM((rows + 3 * EDGE, wide), bf16),
            pltpu.VMEM((rows + 2 * EDGE, wide), bf16),
            pltpu.VMEM((rows + 24, cols), f32),
            pltpu.VMEM((4, LANES, LANES), f32),
            pltpu.VMEM((2, LANES, 2 * LANES), f32),
            pltpu.VMEM((steps * 2 * LANES, 8 * LANES), bf16),
            pltpu.VMEM((2 * LANES, psf_taps * LANES), bf16),
            pltpu.VMEM((8, rows + 2 * EDGE, LANES), f32),
            pltpu.VMEM((psf_taps, rows + EDGE, LANES), f32),
            pltpu.VMEM((rows + EDGE, cols), f32),
            pltpu.VMEM((rows + EDGE, wide), bf16),
            pltpu.VMEM((8, LANES), f32),
            pltpu.VMEM((PIECES, 8, LANES), f32),
            dma((10,)),
            dma((3, chunks)),
            dma((2 * REACH + 1, chunks)),
            dma((chunks,)),
            dma((2, chunks)),
            dma((2,)),
            dma((2,)),
            dma((2, wide // LANES)),
            dma((2, wide // LANES)),
            dma((PIECES - 1,)),
            dma((PIECES,)),
        ],
        compiler_params=pltpu.CompilerParams(
            collective_id=0, has_side_effects=True, vmem_limit_bytes=60 * 1024 * 1024
        ),
        cost_estimate=pl.CostEstimate(
            flops=flops, bytes_accessed=rows * cols * 14, transcendentals=0
        ),
    )(
        owner_map,
        covering,
        row_shift,
        col_shift,
        science,
        template,
        basis_cols,
        basis_rows,
        coeffs,
        psf_kernel,
    )


def solution(mesh):
    return jax.shard_map(
        shards,
        mesh=mesh,
        in_specs=(
            P(("groups", "visit"), None),
            P(("groups", "visit"), None),
            P("groups"),
            P(("groups", "visit"), None),
            P(("groups", "visit"), None),
            P(("groups", "visit"), None),
            P(),
            P(),
            P("groups", None),
            P(),
        ),
        out_specs=(P(("groups", "visit"), None), P(("groups", "visit"), None)),
        check_vma=False,
    )
```

```python
import functools

import jax
import jax.numpy as jnp
from jax import lax
from jax.experimental import pallas as pl
from jax.experimental.pallas import tpu as pltpu
from jax.sharding import PartitionSpec as P

PIECES = 4
REACH = 3
LANES = 128
EDGE = 16
MESH = pl.DeviceIdType.MESH


def kernel(
    devices,
    owner_hbm,
    covering_hbm,
    row_shift_hbm,
    col_shift_hbm,
    science_ref,
    template_ref,
    basis_cols_hbm,
    basis_rows_hbm,
    coeffs_hbm,
    psf_hbm,
    difference_ref,
    detection_ref,
    owner_ref,
    covering_ref,
    row_shift_ref,
    col_shift_ref,
    basis_cols_ref,
    basis_rows_ref,
    coeffs_ref,
    psf_ref,
    own_piece,
    slots_0,
    slots_1,
    slots_2,
    slots_3,
    moved,
    ext,
    ext_low,
    sci_ext,
    small,
    folded,
    weights,
    psf_weights,
    y_model,
    y_psf,
    diff_ext,
    diff_low,
    partial,
    partials,
    fetch,
    piece_send,
    piece_recv,
    relay_send,
    forward_send,
    sci_send,
    sci_recv,
    halo_send,
    halo_recv,
    part_send,
    part_recv,
):
    rows, cols = science_ref.shape
    blocks = cols // LANES
    taps = basis_cols_ref.shape[1]
    basis = basis_cols_ref.shape[0]
    psf_taps = psf_ref.shape[0]
    rim, psf_rim = taps // 2, psf_taps // 2
    f32, bf16 = jnp.float32, jnp.bfloat16

    group = lax.axis_index("groups")
    me = lax.axis_index("visit")
    core = lax.rem(me, 2)
    odd = lax.rem(me // 2, 2)
    sibling = me + 1 - 2 * core
    beside = me + 2 - 4 * odd
    onward = me + 4 - 8 * odd
    held = lax.rem(me + 1, devices)
    visit = held // PIECES
    pos = lax.rem(held, PIECES)
    before = lax.rem(me + devices - 1, devices)
    after = lax.rem(me + 1, devices)
    far = jnp.where(core == 1, me + REACH, me - REACH)
    has_onward = (onward >= 0) & (onward < devices)
    back = me - 4 + 8 * odd
    has_back = (back >= 0) & (back < devices)
    has_far = (far >= 0) & (far < devices)
    has_before, has_after = pos > 0, pos < PIECES - 1

    def peer(step):
        return lax.rem(visit * PIECES + lax.rem(pos + step, PIECES) + devices - 1, devices)

    barrier = pltpu.get_barrier_semaphore()

    def greet(device):
        pl.semaphore_signal(barrier, inc=1, device_id=(group, device), device_id_type=MESH)

    greet(sibling)
    greet(beside)
    for step in range(1, PIECES):
        greet(peer(step))
    pl.when(has_onward)(lambda: greet(onward))
    pl.when(has_back)(lambda: greet(back))
    pl.when(has_far)(lambda: greet(far))
    fetches = [
        pltpu.make_async_copy(src, dst, fetch.at[number])
        for number, (src, dst) in enumerate(
            (
                (owner_hbm, owner_ref),
                (covering_hbm, covering_ref),
                (row_shift_hbm, row_shift_ref),
                (col_shift_hbm, col_shift_ref),
                (basis_cols_hbm, basis_cols_ref),
                (basis_rows_hbm, basis_rows_ref),
                (coeffs_hbm, coeffs_ref),
                (psf_hbm, psf_ref),
                (template_ref, own_piece),
                (science_ref, sci_ext.at[pl.ds(8, rows)]),
            )
        )
    ]
    for copy in fetches:
        copy.start()
    expected = (
        PIECES
        + 1
        + has_onward.astype(jnp.int32)
        + has_back.astype(jnp.int32)
        + has_far.astype(jnp.int32)
    )
    pl.semaphore_wait(barrier, expected)

    def remote(src, dst, send, recv, device):
        return pltpu.make_async_remote_copy(
            src_ref=src,
            dst_ref=dst,
            send_sem=send,
            recv_sem=recv,
            device_id=(group, device),
            device_id_type=MESH,
        )

    slots = (slots_0, slots_1, slots_2, slots_3)
    chunks = len(slots)
    chunk_cols = cols // chunks

    def piece_copy(src, slot, chunk, send, device):
        return remote(src, slots[chunk].at[slot], send, piece_recv.at[slot, chunk], device)

    def own_chunk(chunk):
        return template_ref.at[:, pl.ds(chunk * chunk_cols, chunk_cols)]

    def arrival(slot, chunk):
        return piece_copy(slots[chunk].at[slot], slot, chunk, piece_send.at[0, chunk], sibling)

    beside_slot = 5 - 4 * odd
    back_slot = 1 + 4 * odd
    far_slot = jnp.where(core == 1, 0, 2 * REACH)
    to_beside, to_far, to_sibling, to_onward, from_beside, from_back = [], [], [], [], [], []
    for chunk in range(chunks):
        src = own_chunk(chunk)
        to_beside.append(piece_copy(src, back_slot, chunk, piece_send.at[0, chunk], beside))
        to_far.append(piece_copy(src, far_slot, chunk, piece_send.at[1, chunk], far))
        to_sibling.append(piece_copy(src, 2 + 2 * core, chunk, piece_send.at[2, chunk], sibling))
        beside_chunk, back_chunk = slots[chunk].at[beside_slot], slots[chunk].at[back_slot]
        to_onward.append(piece_copy(beside_chunk, back_slot, chunk, relay_send.at[chunk], onward))
        from_beside.append(
            piece_copy(beside_chunk, beside_slot - 1 + 2 * core, chunk, forward_send.at[0, chunk], sibling)
        )
        from_back.append(
            piece_copy(back_chunk, back_slot - 1 + 2 * core, chunk, forward_send.at[1, chunk], sibling)
        )
    sci_up = remote(
        science_ref.at[pl.ds(0, 8)], sci_ext.at[pl.ds(8 + rows, 8)], sci_send.at[0], sci_recv.at[1], before
    )
    sci_down = remote(
        science_ref.at[pl.ds(rows - 8, 8)], sci_ext.at[pl.ds(0, 8)], sci_send.at[1], sci_recv.at[0], after
    )
    for chunk in range(chunks):
        to_beside[chunk].start()
        pl.when(has_far)(to_far[chunk].start)
        to_sibling[chunk].start()
    pl.when(has_before)(sci_up.start)
    pl.when(has_after)(sci_down.start)
    for copy in fetches:
        copy.wait()

    lane = lax.broadcasted_iota(jnp.int32, (LANES, LANES), 1)
    line_of = lax.broadcasted_iota(jnp.int32, (LANES, LANES), 0)
    reverse = jnp.where(lax.rem(line_of + lane, LANES) == 0, 1.0, 0.0).astype(bf16)
    small[...] = jnp.zeros_like(small)
    small[0, 0:basis, 0:taps] = basis_cols_ref[...]
    small[1, 0:basis, 0:taps] = basis_rows_ref[...]
    small[2, 0:psf_taps, 0:psf_taps] = psf_ref[...]
    small[3, 0:1, 0:basis] = coeffs_ref[pl.ds(visit, 1), :]
    diagonal = line_of == lane
    coeff_col = jnp.sum(
        jnp.where(diagonal, jnp.broadcast_to(small[3, 0:1, :], (LANES, LANES)), 0.0),
        axis=1,
        keepdims=True,
    )
    row_weights = (coeff_col * small[1]).astype(bf16).astype(f32)
    cols_reversed = jnp.dot(small[0].astype(bf16), reverse, preferred_element_type=f32)
    folded[0] = jnp.dot(
        row_weights.T.astype(bf16), cols_reversed.astype(bf16), preferred_element_type=f32
    )
    folded[1] = jnp.dot(small[2].astype(bf16), reverse, preferred_element_type=f32)

    lower = lane <= line_of

    def band(which, index, target, start, s):
        line = folded[which, pl.ds(index, 1), :]
        spread = jnp.broadcast_to(line, (LANES, LANES))
        rolled = pltpu.roll(spread, 0, 1, stride=1, stride_axis=0)
        columns = slice(s * LANES, (s + 1) * LANES)
        target[pl.ds(start, LANES), columns] = jnp.where(lower, rolled, 0.0).astype(bf16)
        target[pl.ds(start + LANES, LANES), columns] = jnp.where(lower, 0.0, rolled).astype(bf16)

    steps = (taps + 7) // 8
    early = min(steps, chunks)

    def pass_on(chunk):
        arrival(beside_slot, chunk).wait_recv()
        pl.when(has_onward)(to_onward[chunk].start)
        from_beside[chunk].start()


    def build(step, carry):
        for chunk in range(early):
            pl.when(step == chunk)(functools.partial(pass_on, chunk))
        start = pl.multiple_of(step * (2 * LANES), 2 * LANES)
        for s in range(8):
            band(0, step * 8 + s, weights, start, s)
        return carry

    lax.fori_loop(0, steps, build, 0)
    for s in range(psf_taps):
        band(1, s, psf_weights, 0, s)

    sci_ext[pl.ds(rows + 16, 8), :] = jnp.zeros((8, cols), f32)
    ext[pl.ds(rows + 2 * EDGE, EDGE), :] = jnp.zeros((EDGE, ext.shape[1]), bf16)
    pad_blocks = (moved.shape[1] - blocks) // 2
    margin = pad_blocks * LANES
    for part in range(pad_blocks):
        for k in range(moved.shape[0]):
            moved[k, part] = jnp.zeros((rows, LANES), f32)
            moved[k, pad_blocks + blocks + part] = jnp.zeros((rows, LANES), f32)
    for part in range(blocks):
        moved[0, pad_blocks + part] = own_piece[:, part * LANES : (part + 1) * LANES].astype(f32)

    @pl.when(jnp.logical_not(has_before))
    def _():
        sci_ext[pl.ds(0, 8), :] = jnp.zeros((8, cols), f32)
        ext[pl.ds(0, EDGE), :] = jnp.zeros((EDGE, ext.shape[1]), bf16)

    @pl.when(jnp.logical_not(has_after))
    def _():
        sci_ext[pl.ds(rows + 8, 8), :] = jnp.zeros((8, cols), f32)
        ext[pl.ds(rows + EDGE, EDGE), :] = jnp.zeros((EDGE, ext.shape[1]), bf16)

    slot_count = moved.shape[0]
    row_to = lax.broadcasted_iota(jnp.int32, (rows, rows), 0)
    row_from = lax.broadcasted_iota(jnp.int32, (rows, rows), 1)
    places, row_offs, col_offs, selects = [None], [None], [0], [None]
    for k in range(1, slot_count):
        holder = owner_ref[covering_ref[0, k]]
        places.append(jnp.clip(holder - me + REACH, 0, 2 * REACH))
        row_offs.append(row_shift_ref[0, k])
        col_offs.append(col_shift_ref[0, k])
        selects.append(jnp.where(row_to - row_from == row_offs[k], 1.0, 0.0).astype(bf16))

    def canvas_block(start, width):
        col = lax.broadcasted_iota(jnp.int32, (1, width), 1) + (start - rim)
        row = lax.broadcasted_iota(jnp.int32, (rows, width), 0)
        total, coverage = None, jnp.ones((rows, width), f32)
        for k in range(slot_count):
            first = margin + start - rim - col_offs[k]
            base = first // LANES if k == 0 else lax.div(first, LANES)
            span = width // LANES + 1
            window = jnp.concatenate([moved[k, base + part] for part in range(span)], axis=1)
            turn = lax.rem(span * LANES - (first - base * LANES), span * LANES)
            placed = pltpu.roll(window, turn, 1)[:, :width]
            total = placed if k == 0 else total + placed
            if k:
                col_old, row_old = col - col_offs[k], row - row_offs[k]
                col_in = jnp.where((col_old >= 0) & (col_old < cols), 1.0, 0.0)
                row_in = jnp.where((row_old >= 0) & (row_old < rows), 1.0, 0.0)
                coverage = coverage + row_in * col_in
        image = jnp.where((col >= 0) & (col < cols), total / coverage, 0.0)
        ext[pl.ds(EDGE, rows), start : start + width] = image.astype(bf16)

    for chunk in range(chunks):
        if early + chunk < chunks:
            pass_on(early + chunk)

        @pl.when(has_back)
        def _():
            arrival(back_slot, chunk).wait_recv()
            from_back[chunk].start()

        for slot in (0, 2, 4, 6):
            origin = me + slot - REACH
            pl.when((origin >= 0) & (origin < devices))(arrival(slot, chunk).wait_recv)
        for k in range(1, slot_count):
            product = jnp.dot(selects[k], slots[chunk][places[k]], preferred_element_type=f32)
            for part in range(chunk_cols // LANES):
                moved[k, pad_blocks + chunk * (chunk_cols // LANES) + part] = product[
                    :, part * LANES : (part + 1) * LANES
                ]
        if chunk:
            canvas_block((chunk - 1) * chunk_cols, chunk_cols)
    canvas_block(cols - chunk_cols, chunk_cols)
    canvas_block(cols, LANES)

    halo_up = remote(
        ext.at[pl.ds(EDGE, EDGE)], ext.at[pl.ds(rows + EDGE, EDGE)], halo_send.at[0], halo_recv.at[1], before
    )
    halo_down = remote(
        ext.at[pl.ds(rows, EDGE)], ext.at[pl.ds(0, EDGE)], halo_send.at[1], halo_recv.at[0], after
    )
    pl.when(has_before)(halo_up.start)
    pl.when(has_after)(halo_down.start)

    @pl.when(has_before)
    def _():
        halo_down.wait_recv()
        sci_down.wait_recv()

    @pl.when(has_after)
    def _():
        halo_up.wait_recv()
        sci_up.wait_recv()

    ext_low[...] = ext[...].astype(f32)[8 : rows + 2 * EDGE + 8].astype(bf16)
    model_rows = rows + 2 * EDGE
    wide_rows = rows + EDGE
    index = lax.broadcasted_iota(jnp.int32, (wide_rows, LANES), 0)
    low_edge = jnp.where(has_before, 0, psf_rim)
    high_edge = jnp.where(has_after, rows + 2 * psf_rim, rows + psf_rim)
    inside = (index >= low_edge) & (index < high_edge)

    def model_block(block, squares):
        start = pl.multiple_of(block * LANES, LANES)
        window = pl.ds(start, 2 * LANES)
        parts = []
        for step in range(steps):
            if step % 2 == 0:
                parts.append(ext[pl.ds(8 * step, model_rows), window])
            else:
                parts.append(ext_low[pl.ds(8 * (step - 1), model_rows), window])
        product = jnp.dot(
            jnp.concatenate(parts, axis=1), weights[...], preferred_element_type=f32
        )
        for s in range(8):
            y_model[s] = product[:, s * LANES : (s + 1) * LANES]
        first = EDGE - rim - psf_rim
        model = y_model[0, pl.ds(first, wide_rows), :]
        for s in range(1, 8):
            model = model + y_model[s, pl.ds(first + s, wide_rows), :]
        diff = sci_ext[pl.ds(8 - psf_rim, wide_rows), pl.ds(start, LANES)] - model
        diff = jnp.where(inside, diff, 0.0)
        diff_ext[:, pl.ds(start, LANES)] = diff
        own = diff[psf_rim : psf_rim + rows]
        difference_ref[:, pl.ds(start, LANES)] = own
        return squares + jnp.sum((own * own).reshape(rows // 8, 8, LANES), axis=0)

    partial[...] = lax.fori_loop(0, blocks, model_block, jnp.zeros((8, LANES), f32))
    part_copies = []
    for step in range(1, PIECES):
        part_copies.append(
            remote(partial, partials.at[pos], part_send.at[step - 1], part_recv.at[pos], peer(step))
        )
    for copy in part_copies:
        copy.start()
    partials[pos] = partial[...]

    tail = jnp.zeros((wide_rows, LANES), f32)
    diff_low[...] = pltpu.roll(jnp.concatenate([diff_ext[...], tail], axis=1), psf_rim, 1).astype(bf16)

    def psf_block(block, carry):
        start = pl.multiple_of(block * LANES, LANES)
        product = jnp.dot(
            diff_low[:, pl.ds(start, 2 * LANES)], psf_weights[...], preferred_element_type=f32
        )
        for s in range(psf_taps):
            y_psf[s] = product[:, s * LANES : (s + 1) * LANES]
        response = y_psf[0, pl.ds(0, rows), :]
        for s in range(1, psf_taps):
            response = response + y_psf[s, pl.ds(s, rows), :]
        detection_ref[:, pl.ds(start, LANES)] = response
        return carry

    lax.fori_loop(0, blocks, psf_block, 0)

    for step in range(1, PIECES):
        source = lax.rem(pos + step, PIECES)
        remote(
            partial, partials.at[source], part_send.at[step - 1], part_recv.at[source], peer(step)
        ).wait_recv()
    variance = jnp.sum(jnp.sum(partials[...], axis=0), keepdims=True) / (PIECES * rows * cols)
    detection_ref[...] = detection_ref[...] / jnp.sqrt(variance + 1e-06)

    for chunk in range(chunks):
        to_beside[chunk].wait_send()
        pl.when(has_far)(to_far[chunk].wait_send)
        to_sibling[chunk].wait_send()
        pl.when(has_onward)(to_onward[chunk].wait_send)
        from_beside[chunk].wait_send()
        pl.when(has_back)(from_back[chunk].wait_send)
    pl.when(has_before)(sci_up.wait_send)
    pl.when(has_after)(sci_down.wait_send)
    pl.when(has_before)(halo_up.wait_send)
    pl.when(has_after)(halo_down.wait_send)
    for copy in part_copies:
        copy.wait_send()


def shards(
    science,
    template,
    owner_map,
    covering,
    row_shift,
    col_shift,
    basis_cols,
    basis_rows,
    coeffs,
    psf_kernel,
):
    rows, cols = science.shape
    devices = lax.axis_size("visit")
    steps = (basis_cols.shape[1] + 7) // 8
    psf_taps = psf_kernel.shape[0]
    f32, bf16 = jnp.float32, jnp.bfloat16
    hbm = pl.BlockSpec(memory_space=pl.ANY)
    chunks = 4
    slot_count = covering.shape[1]
    vmem = pl.BlockSpec(memory_space=pltpu.VMEM)
    wide = cols + LANES
    dma = pltpu.SemaphoreType.DMA
    flops = 2 * cols * (rows + 32) * (2 * LANES) * (8 * steps + psf_taps)
    return pl.pallas_call(
        functools.partial(kernel, devices),
        out_shape=[jax.ShapeDtypeStruct((rows, cols), f32)] * 2,
        in_specs=[hbm] * 10,
        out_specs=[vmem] * 2,
        scratch_shapes=[
            pltpu.SMEM(owner_map.shape, jnp.int32),
            pltpu.SMEM(covering.shape, jnp.int32),
            pltpu.SMEM(row_shift.shape, jnp.int32),
            pltpu.SMEM(col_shift.shape, jnp.int32),
            pltpu.VMEM(basis_cols.shape, f32),
            pltpu.VMEM(basis_rows.shape, f32),
            pltpu.VMEM(coeffs.shape, f32),
            pltpu.VMEM(psf_kernel.shape, f32),
            pltpu.VMEM((rows, cols), bf16),
            *([pltpu.VMEM((2 * REACH + 1, rows, cols // chunks), bf16)] * chunks),
            pltpu.VMEM((slot_count, cols // LANES + 6, rows, LANES), f32),
            pltpu.VMEM((rows + 3 * EDGE, wide), bf16),
            pltpu.VMEM((rows + 2 * EDGE, wide), bf16),
            pltpu.VMEM((rows + 24, cols), f32),
            pltpu.VMEM((4, LANES, LANES), f32),
            pltpu.VMEM((2, LANES, LANES), f32),
            pltpu.VMEM((steps * 2 * LANES, 8 * LANES), bf16),
            pltpu.VMEM((2 * LANES, psf_taps * LANES), bf16),
            pltpu.VMEM((8, rows + 2 * EDGE, LANES), f32),
            pltpu.VMEM((psf_taps, rows + EDGE, LANES), f32),
            pltpu.VMEM((rows + EDGE, cols), f32),
            pltpu.VMEM((rows + EDGE, wide), bf16),
            pltpu.VMEM((8, LANES), f32),
            pltpu.VMEM((PIECES, 8, LANES), f32),
            dma((10,)),
            dma((3, chunks)),
            dma((2 * REACH + 1, chunks)),
            dma((chunks,)),
            dma((2, chunks)),
            dma((2,)),
            dma((2,)),
            dma((2,)),
            dma((2,)),
            dma((PIECES - 1,)),
            dma((PIECES,)),
        ],
        compiler_params=pltpu.CompilerParams(
            collective_id=0, has_side_effects=True, vmem_limit_bytes=60 * 1024 * 1024
        ),
        cost_estimate=pl.CostEstimate(
            flops=flops, bytes_accessed=rows * cols * 14, transcendentals=0
        ),
    )(
        owner_map,
        covering,
        row_shift,
        col_shift,
        science,
        template,
        basis_cols,
        basis_rows,
        coeffs,
        psf_kernel,
    )


def solution(mesh):
    return jax.shard_map(
        shards,
        mesh=mesh,
        in_specs=(
            P(("groups", "visit"), None),
            P(("groups", "visit"), None),
            P("groups"),
            P(("groups", "visit"), None),
            P(("groups", "visit"), None),
            P(("groups", "visit"), None),
            P(),
            P(),
            P("groups", None),
            P(),
        ),
        out_specs=(P(("groups", "visit"), None), P(("groups", "visit"), None)),
        check_vma=False,
    )
```

```python
import functools

import jax
import jax.numpy as jnp
from jax import lax
from jax.experimental import pallas as pl
from jax.experimental.pallas import tpu as pltpu
from jax.sharding import PartitionSpec as P

PIECES = 4
REACH = 3
LANES = 128
EDGE = 16
MESH = pl.DeviceIdType.MESH


def kernel(
    devices,
    owner_hbm,
    covering_hbm,
    row_shift_hbm,
    col_shift_hbm,
    science_ref,
    template_ref,
    basis_cols_hbm,
    basis_rows_hbm,
    coeffs_hbm,
    psf_hbm,
    difference_hbm,
    detection_hbm,
    difference_ref,
    detection_ref,
    owner_ref,
    covering_ref,
    row_shift_ref,
    col_shift_ref,
    basis_cols_ref,
    basis_rows_ref,
    coeffs_ref,
    psf_ref,
    own_piece,
    slots_0,
    slots_1,
    slots_2,
    slots_3,
    moved,
    ext,
    ext_low,
    sci_ext,
    small,
    folded,
    weights,
    psf_weights,
    y_model,
    y_psf,
    diff_ext,
    diff_low,
    partial,
    partials,
    fetch,
    piece_send,
    piece_recv,
    relay_send,
    forward_send,
    sci_send,
    sci_recv,
    halo_send,
    halo_recv,
    part_send,
    part_recv,
    out_sem,
):
    rows, cols = science_ref.shape
    blocks = cols // LANES
    taps = basis_cols_ref.shape[1]
    basis = basis_cols_ref.shape[0]
    psf_taps = psf_ref.shape[0]
    rim, psf_rim = taps // 2, psf_taps // 2
    f32, bf16 = jnp.float32, jnp.bfloat16

    group = lax.axis_index("groups")
    me = lax.axis_index("visit")
    core = lax.rem(me, 2)
    odd = lax.rem(me // 2, 2)
    sibling = me + 1 - 2 * core
    beside = me + 2 - 4 * odd
    onward = me + 4 - 8 * odd
    held = lax.rem(me + 1, devices)
    visit = held // PIECES
    pos = lax.rem(held, PIECES)
    before = lax.rem(me + devices - 1, devices)
    after = lax.rem(me + 1, devices)
    far = jnp.where(core == 1, me + REACH, me - REACH)
    has_onward = (onward >= 0) & (onward < devices)
    back = me - 4 + 8 * odd
    has_back = (back >= 0) & (back < devices)
    has_far = (far >= 0) & (far < devices)
    has_before, has_after = pos > 0, pos < PIECES - 1

    def peer(step):
        return lax.rem(visit * PIECES + lax.rem(pos + step, PIECES) + devices - 1, devices)

    barrier = pltpu.get_barrier_semaphore()

    def greet(device):
        pl.semaphore_signal(barrier, inc=1, device_id=(group, device), device_id_type=MESH)

    greet(sibling)
    greet(beside)
    for step in range(1, PIECES):
        greet(peer(step))
    pl.when(has_onward)(lambda: greet(onward))
    pl.when(has_back)(lambda: greet(back))
    pl.when(has_far)(lambda: greet(far))
    fetches = [
        pltpu.make_async_copy(src, dst, fetch.at[number])
        for number, (src, dst) in enumerate(
            (
                (owner_hbm, owner_ref),
                (covering_hbm, covering_ref),
                (row_shift_hbm, row_shift_ref),
                (col_shift_hbm, col_shift_ref),
                (basis_cols_hbm, basis_cols_ref),
                (basis_rows_hbm, basis_rows_ref),
                (coeffs_hbm, coeffs_ref),
                (psf_hbm, psf_ref),
                (template_ref, own_piece),
                (science_ref, sci_ext.at[pl.ds(8, rows)]),
            )
        )
    ]
    for copy in fetches:
        copy.start()
    expected = (
        PIECES
        + 1
        + has_onward.astype(jnp.int32)
        + has_back.astype(jnp.int32)
        + has_far.astype(jnp.int32)
    )
    pl.semaphore_wait(barrier, expected)

    def remote(src, dst, send, recv, device):
        return pltpu.make_async_remote_copy(
            src_ref=src,
            dst_ref=dst,
            send_sem=send,
            recv_sem=recv,
            device_id=(group, device),
            device_id_type=MESH,
        )

    slots = (slots_0, slots_1, slots_2, slots_3)
    chunks = len(slots)
    chunk_cols = cols // chunks

    def piece_copy(src, slot, chunk, send, device):
        return remote(src, slots[chunk].at[slot], send, piece_recv.at[slot, chunk], device)

    def own_chunk(chunk):
        return template_ref.at[:, pl.ds(chunk * chunk_cols, chunk_cols)]

    def arrival(slot, chunk):
        return piece_copy(slots[chunk].at[slot], slot, chunk, piece_send.at[0, chunk], sibling)

    beside_slot = 5 - 4 * odd
    back_slot = 1 + 4 * odd
    far_slot = jnp.where(core == 1, 0, 2 * REACH)
    to_beside, to_far, to_sibling, to_onward, from_beside, from_back = [], [], [], [], [], []
    for chunk in range(chunks):
        src = own_chunk(chunk)
        to_beside.append(piece_copy(src, back_slot, chunk, piece_send.at[0, chunk], beside))
        to_far.append(piece_copy(src, far_slot, chunk, piece_send.at[1, chunk], far))
        to_sibling.append(piece_copy(src, 2 + 2 * core, chunk, piece_send.at[2, chunk], sibling))
        beside_chunk, back_chunk = slots[chunk].at[beside_slot], slots[chunk].at[back_slot]
        to_onward.append(piece_copy(beside_chunk, back_slot, chunk, relay_send.at[chunk], onward))
        from_beside.append(
            piece_copy(beside_chunk, beside_slot - 1 + 2 * core, chunk, forward_send.at[0, chunk], sibling)
        )
        from_back.append(
            piece_copy(back_chunk, back_slot - 1 + 2 * core, chunk, forward_send.at[1, chunk], sibling)
        )
    sci_up = remote(
        science_ref.at[pl.ds(0, 8)], sci_ext.at[pl.ds(8 + rows, 8)], sci_send.at[0], sci_recv.at[1], before
    )
    sci_down = remote(
        science_ref.at[pl.ds(rows - 8, 8)], sci_ext.at[pl.ds(0, 8)], sci_send.at[1], sci_recv.at[0], after
    )
    for chunk in range(chunks):
        to_beside[chunk].start()
        pl.when(has_far)(to_far[chunk].start)
        to_sibling[chunk].start()
    pl.when(has_before)(sci_up.start)
    pl.when(has_after)(sci_down.start)
    for copy in fetches:
        copy.wait()

    lane = lax.broadcasted_iota(jnp.int32, (LANES, LANES), 1)
    line_of = lax.broadcasted_iota(jnp.int32, (LANES, LANES), 0)
    reverse = jnp.where(lax.rem(line_of + lane, LANES) == 0, 1.0, 0.0).astype(bf16)
    small[...] = jnp.zeros_like(small)
    small[0, 0:basis, 0:taps] = basis_cols_ref[...]
    small[1, 0:basis, 0:taps] = basis_rows_ref[...]
    small[2, 0:psf_taps, 0:psf_taps] = psf_ref[...]
    small[3, 0:1, 0:basis] = coeffs_ref[pl.ds(visit, 1), :]
    diagonal = line_of == lane
    coeff_col = jnp.sum(
        jnp.where(diagonal, jnp.broadcast_to(small[3, 0:1, :], (LANES, LANES)), 0.0),
        axis=1,
        keepdims=True,
    )
    row_weights = (coeff_col * small[1]).astype(bf16).astype(f32)
    cols_reversed = jnp.dot(small[0].astype(bf16), reverse, preferred_element_type=f32)
    folded[0] = jnp.dot(
        row_weights.T.astype(bf16), cols_reversed.astype(bf16), preferred_element_type=f32
    )
    folded[1] = jnp.dot(small[2].astype(bf16), reverse, preferred_element_type=f32)

    lower = lane <= line_of

    def band(which, index, target, start, s):
        line = folded[which, pl.ds(index, 1), :]
        spread = jnp.broadcast_to(line, (LANES, LANES))
        rolled = pltpu.roll(spread, 0, 1, stride=1, stride_axis=0)
        columns = slice(s * LANES, (s + 1) * LANES)
        target[pl.ds(start, LANES), columns] = jnp.where(lower, rolled, 0.0).astype(bf16)
        target[pl.ds(start + LANES, LANES), columns] = jnp.where(lower, 0.0, rolled).astype(bf16)

    steps = (taps + 7) // 8
    early = min(steps, chunks)

    def pass_on(chunk):
        arrival(beside_slot, chunk).wait_recv()
        pl.when(has_onward)(to_onward[chunk].start)
        from_beside[chunk].start()


    def build(step, carry):
        for chunk in range(early):
            pl.when(step == chunk)(functools.partial(pass_on, chunk))
        start = pl.multiple_of(step * (2 * LANES), 2 * LANES)
        for s in range(8):
            band(0, step * 8 + s, weights, start, s)
        return carry

    lax.fori_loop(0, steps, build, 0)
    for s in range(psf_taps):
        band(1, s, psf_weights, 0, s)

    sci_ext[pl.ds(rows + 16, 8), :] = jnp.zeros((8, cols), f32)
    ext[pl.ds(rows + 2 * EDGE, EDGE), :] = jnp.zeros((EDGE, ext.shape[1]), bf16)
    pad_blocks = (moved.shape[1] - blocks) // 2
    margin = pad_blocks * LANES
    for part in range(pad_blocks):
        for k in range(moved.shape[0]):
            moved[k, part] = jnp.zeros((rows, LANES), f32)
            moved[k, pad_blocks + blocks + part] = jnp.zeros((rows, LANES), f32)
    for part in range(blocks):
        moved[0, pad_blocks + part] = own_piece[:, part * LANES : (part + 1) * LANES].astype(f32)

    @pl.when(jnp.logical_not(has_before))
    def _():
        sci_ext[pl.ds(0, 8), :] = jnp.zeros((8, cols), f32)
        ext[pl.ds(0, EDGE), :] = jnp.zeros((EDGE, ext.shape[1]), bf16)

    @pl.when(jnp.logical_not(has_after))
    def _():
        sci_ext[pl.ds(rows + 8, 8), :] = jnp.zeros((8, cols), f32)
        ext[pl.ds(rows + EDGE, EDGE), :] = jnp.zeros((EDGE, ext.shape[1]), bf16)

    slot_count = moved.shape[0]
    row_to = lax.broadcasted_iota(jnp.int32, (rows, rows), 0)
    row_from = lax.broadcasted_iota(jnp.int32, (rows, rows), 1)
    places, row_offs, col_offs, selects = [None], [None], [0], [None]
    for k in range(1, slot_count):
        holder = owner_ref[covering_ref[0, k]]
        places.append(jnp.clip(holder - me + REACH, 0, 2 * REACH))
        row_offs.append(row_shift_ref[0, k])
        col_offs.append(col_shift_ref[0, k])
        selects.append(jnp.where(row_to - row_from == row_offs[k], 1.0, 0.0).astype(bf16))

    def canvas_block(start, width):
        col = lax.broadcasted_iota(jnp.int32, (1, width), 1) + (start - rim)
        row = lax.broadcasted_iota(jnp.int32, (rows, width), 0)
        total, coverage = None, jnp.ones((rows, width), f32)
        for k in range(slot_count):
            first = margin + start - rim - col_offs[k]
            base = first // LANES if k == 0 else lax.div(first, LANES)
            span = width // LANES + 1
            window = jnp.concatenate([moved[k, base + part] for part in range(span)], axis=1)
            turn = lax.rem(span * LANES - (first - base * LANES), span * LANES)
            placed = pltpu.roll(window, turn, 1)[:, :width]
            total = placed if k == 0 else total + placed
            if k:
                col_old, row_old = col - col_offs[k], row - row_offs[k]
                col_in = jnp.where((col_old >= 0) & (col_old < cols), 1.0, 0.0)
                row_in = jnp.where((row_old >= 0) & (row_old < rows), 1.0, 0.0)
                coverage = coverage + row_in * col_in
        image = jnp.where((col >= 0) & (col < cols), total / coverage, 0.0)
        ext[pl.ds(EDGE, rows), start : start + width] = image.astype(bf16)

    spans = [(chunk * chunk_cols, chunk_cols) for chunk in range(chunks)] + [(cols, LANES)]
    halos = []
    for number, (start, width) in enumerate(spans):
        columns = pl.ds(start, width)
        up = remote(
            ext.at[pl.ds(EDGE, EDGE), columns],
            ext.at[pl.ds(rows + EDGE, EDGE), columns],
            halo_send.at[0, number],
            halo_recv.at[1, number],
            before,
        )
        down = remote(
            ext.at[pl.ds(rows, EDGE), columns],
            ext.at[pl.ds(0, EDGE), columns],
            halo_send.at[1, number],
            halo_recv.at[0, number],
            after,
        )
        halos.append((up, down))

    def canvas_and_halo(number):
        canvas_block(*spans[number])
        pl.when(has_before)(halos[number][0].start)
        pl.when(has_after)(halos[number][1].start)

    def finish_span(number):
        pl.when(has_before)(halos[number][1].wait_recv)
        pl.when(has_after)(halos[number][0].wait_recv)
        start, width = spans[number]
        columns = slice(start, start + width)
        ext_low[:, columns] = ext[:, columns].astype(f32)[8 : rows + 2 * EDGE + 8].astype(bf16)

    for chunk in range(chunks):
        if early + chunk < chunks:
            pass_on(early + chunk)

        @pl.when(has_back)
        def _():
            arrival(back_slot, chunk).wait_recv()
            from_back[chunk].start()

        for slot in (0, 2, 4, 6):
            origin = me + slot - REACH
            pl.when((origin >= 0) & (origin < devices))(arrival(slot, chunk).wait_recv)
        for k in range(1, slot_count):
            product = jnp.dot(selects[k], slots[chunk][places[k]], preferred_element_type=f32)
            for part in range(chunk_cols // LANES):
                moved[k, pad_blocks + chunk * (chunk_cols // LANES) + part] = product[
                    :, part * LANES : (part + 1) * LANES
                ]
        if chunk:
            canvas_and_halo(chunk - 1)
    canvas_and_halo(chunks - 1)
    canvas_and_halo(chunks)

    model_rows = rows + 2 * EDGE
    wide_rows = rows + EDGE
    index = lax.broadcasted_iota(jnp.int32, (wide_rows, LANES), 0)
    low_edge = jnp.where(has_before, 0, psf_rim)
    high_edge = jnp.where(has_after, rows + 2 * psf_rim, rows + psf_rim)
    inside = (index >= low_edge) & (index < high_edge)

    def model_block(block, squares):
        start = pl.multiple_of(block * LANES, LANES)
        window = pl.ds(start, 2 * LANES)
        parts = []
        for step in range(steps):
            if step % 2 == 0:
                parts.append(ext[pl.ds(8 * step, model_rows), window])
            else:
                parts.append(ext_low[pl.ds(8 * (step - 1), model_rows), window])
        product = jnp.dot(
            jnp.concatenate(parts, axis=1), weights[...], preferred_element_type=f32
        )
        for s in range(8):
            y_model[s] = product[:, s * LANES : (s + 1) * LANES]
        first = EDGE - rim - psf_rim
        model = y_model[0, pl.ds(first, wide_rows), :]
        for s in range(1, 8):
            model = model + y_model[s, pl.ds(first + s, wide_rows), :]
        diff = sci_ext[pl.ds(8 - psf_rim, wide_rows), pl.ds(start, LANES)] - model
        diff = jnp.where(inside, diff, 0.0)
        diff_ext[:, pl.ds(start, LANES)] = diff
        own = diff[psf_rim : psf_rim + rows]
        difference_ref[:, pl.ds(start, LANES)] = own
        return squares + jnp.sum((own * own).reshape(rows // 8, 8, LANES), axis=0)

    pl.when(has_before)(sci_down.wait_recv)
    pl.when(has_after)(sci_up.wait_recv)
    ready = chunks // 2
    for number in range(ready):
        finish_span(number)
    first_blocks = ready * chunk_cols // LANES - 1
    squares = lax.fori_loop(0, first_blocks, model_block, jnp.zeros((8, LANES), f32))
    for number in range(ready, chunks + 1):
        finish_span(number)
    partial[...] = lax.fori_loop(first_blocks, blocks, model_block, squares)
    difference_copy = pltpu.make_async_copy(difference_ref, difference_hbm, out_sem.at[0])
    difference_copy.start()
    part_copies = []
    for step in range(1, PIECES):
        part_copies.append(
            remote(partial, partials.at[pos], part_send.at[step - 1], part_recv.at[pos], peer(step))
        )
    for copy in part_copies:
        copy.start()
    partials[pos] = partial[...]

    tail = jnp.zeros((wide_rows, LANES), f32)
    diff_low[...] = pltpu.roll(jnp.concatenate([diff_ext[...], tail], axis=1), psf_rim, 1).astype(bf16)

    def psf_block(block, carry):
        start = pl.multiple_of(block * LANES, LANES)
        product = jnp.dot(
            diff_low[:, pl.ds(start, 2 * LANES)], psf_weights[...], preferred_element_type=f32
        )
        for s in range(psf_taps):
            y_psf[s] = product[:, s * LANES : (s + 1) * LANES]
        response = y_psf[0, pl.ds(0, rows), :]
        for s in range(1, psf_taps):
            response = response + y_psf[s, pl.ds(s, rows), :]
        detection_ref[:, pl.ds(start, LANES)] = response
        return carry

    lax.fori_loop(0, blocks, psf_block, 0)

    for step in range(1, PIECES):
        source = lax.rem(pos + step, PIECES)
        remote(
            partial, partials.at[source], part_send.at[step - 1], part_recv.at[source], peer(step)
        ).wait_recv()
    variance = jnp.sum(jnp.sum(partials[...], axis=0), keepdims=True) / (PIECES * rows * cols)
    detection_ref[...] = detection_ref[...] / jnp.sqrt(variance + 1e-06)
    detection_copy = pltpu.make_async_copy(detection_ref, detection_hbm, out_sem.at[1])
    detection_copy.start()

    for chunk in range(chunks):
        to_beside[chunk].wait_send()
        pl.when(has_far)(to_far[chunk].wait_send)
        to_sibling[chunk].wait_send()
        pl.when(has_onward)(to_onward[chunk].wait_send)
        from_beside[chunk].wait_send()
        pl.when(has_back)(from_back[chunk].wait_send)
    pl.when(has_before)(sci_up.wait_send)
    pl.when(has_after)(sci_down.wait_send)
    for up, down in halos:
        pl.when(has_before)(up.wait_send)
        pl.when(has_after)(down.wait_send)
    difference_copy.wait()
    detection_copy.wait()
    for copy in part_copies:
        copy.wait_send()


def hand_out(difference, detection, difference_out, detection_out, sem):
    parts = sem.shape[1]
    size = difference.shape[0] // parts
    copies = []
    for number, (src, dst) in enumerate(((difference, difference_out), (detection, detection_out))):
        for part in range(parts):
            span = pl.ds(part * size, size)
            copies.append(pltpu.make_async_copy(src.at[span], dst.at[span], sem.at[number, part]))
    for copy in copies:
        copy.start()
    for copy in copies:
        copy.wait()


def shards(
    science,
    template,
    owner_map,
    covering,
    row_shift,
    col_shift,
    basis_cols,
    basis_rows,
    coeffs,
    psf_kernel,
):
    rows, cols = science.shape
    devices = lax.axis_size("visit")
    steps = (basis_cols.shape[1] + 7) // 8
    psf_taps = psf_kernel.shape[0]
    f32, bf16 = jnp.float32, jnp.bfloat16
    hbm = pl.BlockSpec(memory_space=pl.ANY)
    chunks = 4
    slot_count = covering.shape[1]
    wide = cols + LANES
    dma = pltpu.SemaphoreType.DMA
    flops = 2 * cols * (rows + 32) * (2 * LANES) * (8 * steps + psf_taps)
    results = pl.pallas_call(
        functools.partial(kernel, devices),
        out_shape=[jax.ShapeDtypeStruct((rows, cols), f32)] * 2,
        in_specs=[hbm] * 10,
        out_specs=[hbm] * 2,
        scratch_shapes=[
            pltpu.VMEM((rows, cols), f32),
            pltpu.VMEM((rows, cols), f32),
            pltpu.SMEM(owner_map.shape, jnp.int32),
            pltpu.SMEM(covering.shape, jnp.int32),
            pltpu.SMEM(row_shift.shape, jnp.int32),
            pltpu.SMEM(col_shift.shape, jnp.int32),
            pltpu.VMEM(basis_cols.shape, f32),
            pltpu.VMEM(basis_rows.shape, f32),
            pltpu.VMEM(coeffs.shape, f32),
            pltpu.VMEM(psf_kernel.shape, f32),
            pltpu.VMEM((rows, cols), bf16),
            *([pltpu.VMEM((2 * REACH + 1, rows, cols // chunks), bf16)] * chunks),
            pltpu.VMEM((slot_count, cols // LANES + 6, rows, LANES), f32),
            pltpu.VMEM((rows + 3 * EDGE, wide), bf16),
            pltpu.VMEM((rows + 2 * EDGE, wide), bf16),
            pltpu.VMEM((rows + 24, cols), f32),
            pltpu.VMEM((4, LANES, LANES), f32),
            pltpu.VMEM((2, LANES, LANES), f32),
            pltpu.VMEM((steps * 2 * LANES, 8 * LANES), bf16),
            pltpu.VMEM((2 * LANES, psf_taps * LANES), bf16),
            pltpu.VMEM((8, rows + 2 * EDGE, LANES), f32),
            pltpu.VMEM((psf_taps, rows + EDGE, LANES), f32),
            pltpu.VMEM((rows + EDGE, cols), f32),
            pltpu.VMEM((rows + EDGE, wide), bf16),
            pltpu.VMEM((8, LANES), f32),
            pltpu.VMEM((PIECES, 8, LANES), f32),
            dma((10,)),
            dma((3, chunks)),
            dma((2 * REACH + 1, chunks)),
            dma((chunks,)),
            dma((2, chunks)),
            dma((2,)),
            dma((2,)),
            dma((2, chunks + 1)),
            dma((2, chunks + 1)),
            dma((PIECES - 1,)),
            dma((PIECES,)),
            dma((2,)),
        ],
        compiler_params=pltpu.CompilerParams(
            collective_id=0, has_side_effects=True, vmem_limit_bytes=60 * 1024 * 1024
        ),
        cost_estimate=pl.CostEstimate(
            flops=flops, bytes_accessed=rows * cols * 14, transcendentals=0
        ),
    )(
        owner_map,
        covering,
        row_shift,
        col_shift,
        science,
        template,
        basis_cols,
        basis_rows,
        coeffs,
        psf_kernel,
    )
    return pl.pallas_call(
        hand_out,
        out_shape=[jax.ShapeDtypeStruct((rows, cols), f32)] * 2,
        in_specs=[hbm] * 2,
        out_specs=[hbm] * 2,
        scratch_shapes=[dma((2, 4))],
        compiler_params=pltpu.CompilerParams(vmem_limit_bytes=60 * 1024 * 1024),
        cost_estimate=pl.CostEstimate(flops=0, bytes_accessed=rows * cols * 16, transcendentals=0),
    )(*results)


def solution(mesh):
    return jax.shard_map(
        shards,
        mesh=mesh,
        in_specs=(
            P(("groups", "visit"), None),
            P(("groups", "visit"), None),
            P("groups"),
            P(("groups", "visit"), None),
            P(("groups", "visit"), None),
            P(("groups", "visit"), None),
            P(),
            P(),
            P("groups", None),
            P(),
        ),
        out_specs=(P(("groups", "visit"), None), P(("groups", "visit"), None)),
        check_vma=False,
    )
```

```python
import functools

import jax
import jax.numpy as jnp
from jax import lax
from jax.experimental import pallas as pl
from jax.experimental.pallas import tpu as pltpu
from jax.sharding import PartitionSpec as P

PIECES = 4
REACH = 3
LANES = 128
EDGE = 16
MESH = pl.DeviceIdType.MESH


def kernel(
    devices,
    owner_hbm,
    covering_hbm,
    row_shift_hbm,
    col_shift_hbm,
    science_ref,
    template_ref,
    basis_cols_hbm,
    basis_rows_hbm,
    coeffs_hbm,
    psf_hbm,
    difference_hbm,
    detection_hbm,
    difference_ref,
    detection_ref,
    owner_ref,
    covering_ref,
    row_shift_ref,
    col_shift_ref,
    basis_cols_ref,
    basis_rows_ref,
    coeffs_ref,
    psf_ref,
    own_piece,
    slots_0,
    slots_1,
    slots_2,
    slots_3,
    moved,
    ext,
    ext_low,
    sci_ext,
    small,
    folded,
    weights,
    psf_weights,
    y_model,
    y_psf,
    diff_ext,
    diff_low,
    partial,
    partials,
    fetch,
    piece_send,
    piece_recv,
    relay_send,
    forward_send,
    sci_send,
    sci_recv,
    halo_send,
    halo_recv,
    part_send,
    part_recv,
    out_sem,
):
    rows, cols = science_ref.shape
    blocks = cols // LANES
    taps = basis_cols_ref.shape[1]
    basis = basis_cols_ref.shape[0]
    psf_taps = psf_ref.shape[0]
    rim, psf_rim = taps // 2, psf_taps // 2
    f32, bf16 = jnp.float32, jnp.bfloat16

    group = lax.axis_index("groups")
    me = lax.axis_index("visit")
    core = lax.rem(me, 2)
    odd = lax.rem(me // 2, 2)
    sibling = me + 1 - 2 * core
    beside = me + 2 - 4 * odd
    onward = me + 4 - 8 * odd
    held = lax.rem(me + 1, devices)
    visit = held // PIECES
    pos = lax.rem(held, PIECES)
    before = lax.rem(me + devices - 1, devices)
    after = lax.rem(me + 1, devices)
    far = jnp.where(core == 1, me + REACH, me - REACH)
    has_onward = (onward >= 0) & (onward < devices)
    back = me - 4 + 8 * odd
    has_back = (back >= 0) & (back < devices)
    has_far = (far >= 0) & (far < devices)
    has_before, has_after = pos > 0, pos < PIECES - 1

    def peer(step):
        return lax.rem(visit * PIECES + lax.rem(pos + step, PIECES) + devices - 1, devices)

    barrier = pltpu.get_barrier_semaphore()

    def greet(device):
        pl.semaphore_signal(barrier, inc=1, device_id=(group, device), device_id_type=MESH)

    greet(sibling)
    greet(beside)
    for step in range(1, PIECES):
        greet(peer(step))
    pl.when(has_onward)(lambda: greet(onward))
    pl.when(has_back)(lambda: greet(back))
    pl.when(has_far)(lambda: greet(far))
    fetches = [
        pltpu.make_async_copy(src, dst, fetch.at[number])
        for number, (src, dst) in enumerate(
            (
                (owner_hbm, owner_ref),
                (covering_hbm, covering_ref),
                (row_shift_hbm, row_shift_ref),
                (col_shift_hbm, col_shift_ref),
                (basis_cols_hbm, basis_cols_ref),
                (basis_rows_hbm, basis_rows_ref),
                (coeffs_hbm, coeffs_ref),
                (psf_hbm, psf_ref),
                (template_ref, own_piece),
                (science_ref, sci_ext.at[pl.ds(8, rows)]),
            )
        )
    ]
    for copy in fetches:
        copy.start()
    expected = (
        PIECES
        + 1
        + has_onward.astype(jnp.int32)
        + has_back.astype(jnp.int32)
        + has_far.astype(jnp.int32)
    )
    pl.semaphore_wait(barrier, expected)

    def remote(src, dst, send, recv, device):
        return pltpu.make_async_remote_copy(
            src_ref=src,
            dst_ref=dst,
            send_sem=send,
            recv_sem=recv,
            device_id=(group, device),
            device_id_type=MESH,
        )

    slots = (slots_0, slots_1, slots_2, slots_3)
    chunks = len(slots)
    chunk_cols = cols // chunks

    def piece_copy(src, slot, chunk, send, device):
        return remote(src, slots[chunk].at[slot], send, piece_recv.at[slot, chunk], device)

    def own_chunk(chunk):
        return template_ref.at[:, pl.ds(chunk * chunk_cols, chunk_cols)]

    def arrival(slot, chunk):
        return piece_copy(slots[chunk].at[slot], slot, chunk, piece_send.at[0, chunk], sibling)

    beside_slot = 5 - 4 * odd
    back_slot = 1 + 4 * odd
    far_slot = jnp.where(core == 1, 0, 2 * REACH)
    to_beside, to_far, to_sibling, to_onward, from_beside, from_back = [], [], [], [], [], []
    for chunk in range(chunks):
        src = own_chunk(chunk)
        to_beside.append(piece_copy(src, back_slot, chunk, piece_send.at[0, chunk], beside))
        to_far.append(piece_copy(src, far_slot, chunk, piece_send.at[1, chunk], far))
        to_sibling.append(piece_copy(src, 2 + 2 * core, chunk, piece_send.at[2, chunk], sibling))
        beside_chunk, back_chunk = slots[chunk].at[beside_slot], slots[chunk].at[back_slot]
        to_onward.append(piece_copy(beside_chunk, back_slot, chunk, relay_send.at[chunk], onward))
        from_beside.append(
            piece_copy(beside_chunk, beside_slot - 1 + 2 * core, chunk, forward_send.at[0, chunk], sibling)
        )
        from_back.append(
            piece_copy(back_chunk, back_slot - 1 + 2 * core, chunk, forward_send.at[1, chunk], sibling)
        )
    sci_up = remote(
        science_ref.at[pl.ds(0, 8)], sci_ext.at[pl.ds(8 + rows, 8)], sci_send.at[0], sci_recv.at[1], before
    )
    sci_down = remote(
        science_ref.at[pl.ds(rows - 8, 8)], sci_ext.at[pl.ds(0, 8)], sci_send.at[1], sci_recv.at[0], after
    )
    for chunk in range(chunks):
        to_beside[chunk].start()
        pl.when(has_far)(to_far[chunk].start)
        to_sibling[chunk].start()
    pl.when(has_before)(sci_up.start)
    pl.when(has_after)(sci_down.start)
    for copy in fetches:
        copy.wait()

    lane = lax.broadcasted_iota(jnp.int32, (LANES, LANES), 1)
    line_of = lax.broadcasted_iota(jnp.int32, (LANES, LANES), 0)
    reverse = jnp.where(lax.rem(line_of + lane, LANES) == 0, 1.0, 0.0).astype(bf16)
    small[...] = jnp.zeros_like(small)
    small[0, 0:basis, 0:taps] = basis_cols_ref[...]
    small[1, 0:basis, 0:taps] = basis_rows_ref[...]
    small[2, 0:psf_taps, 0:psf_taps] = psf_ref[...]
    small[3, 0:1, 0:basis] = coeffs_ref[pl.ds(visit, 1), :]
    diagonal = line_of == lane
    coeff_col = jnp.sum(
        jnp.where(diagonal, jnp.broadcast_to(small[3, 0:1, :], (LANES, LANES)), 0.0),
        axis=1,
        keepdims=True,
    )
    row_weights = (coeff_col * small[1]).astype(bf16).astype(f32)
    cols_reversed = jnp.dot(small[0].astype(bf16), reverse, preferred_element_type=f32)
    folded[0] = jnp.dot(
        row_weights.T.astype(bf16), cols_reversed.astype(bf16), preferred_element_type=f32
    )
    folded[1] = jnp.dot(small[2].astype(bf16), reverse, preferred_element_type=f32)

    lower = lane <= line_of

    def band(which, index, target, start, s):
        line = folded[which, pl.ds(index, 1), :]
        spread = jnp.broadcast_to(line, (LANES, LANES))
        rolled = pltpu.roll(spread, 0, 1, stride=1, stride_axis=0)
        columns = slice(s * LANES, (s + 1) * LANES)
        target[pl.ds(start, LANES), columns] = jnp.where(lower, rolled, 0.0).astype(bf16)
        target[pl.ds(start + LANES, LANES), columns] = jnp.where(lower, 0.0, rolled).astype(bf16)

    steps = (taps + 7) // 8
    early = min(steps, chunks)

    def pass_on(chunk):
        arrival(beside_slot, chunk).wait_recv()
        pl.when(has_onward)(to_onward[chunk].start)
        from_beside[chunk].start()


    def build(step, carry):
        for chunk in range(early):
            pl.when(step == chunk)(functools.partial(pass_on, chunk))
        start = pl.multiple_of(step * (2 * LANES), 2 * LANES)
        for s in range(8):
            band(0, step * 8 + s, weights, start, s)
        return carry

    lax.fori_loop(0, steps, build, 0)
    for s in range(psf_taps):
        band(1, s, psf_weights, 0, s)

    sci_ext[pl.ds(rows + 16, 8), :] = jnp.zeros((8, cols), f32)
    ext[pl.ds(rows + 2 * EDGE, EDGE), :] = jnp.zeros((EDGE, ext.shape[1]), bf16)
    pad_blocks = (moved.shape[1] - blocks) // 2
    margin = pad_blocks * LANES
    for part in range(pad_blocks):
        for k in range(moved.shape[0]):
            moved[k, part] = jnp.zeros((rows, LANES), f32)
            moved[k, pad_blocks + blocks + part] = jnp.zeros((rows, LANES), f32)
    for part in range(blocks):
        moved[0, pad_blocks + part] = own_piece[:, part * LANES : (part + 1) * LANES].astype(f32)

    @pl.when(jnp.logical_not(has_before))
    def _():
        sci_ext[pl.ds(0, 8), :] = jnp.zeros((8, cols), f32)
        ext[pl.ds(0, EDGE), :] = jnp.zeros((EDGE, ext.shape[1]), bf16)

    @pl.when(jnp.logical_not(has_after))
    def _():
        sci_ext[pl.ds(rows + 8, 8), :] = jnp.zeros((8, cols), f32)
        ext[pl.ds(rows + EDGE, EDGE), :] = jnp.zeros((EDGE, ext.shape[1]), bf16)

    slot_count = moved.shape[0]
    row_to = lax.broadcasted_iota(jnp.int32, (rows, rows), 0)
    row_from = lax.broadcasted_iota(jnp.int32, (rows, rows), 1)
    places, row_offs, col_offs, selects = [None], [None], [0], [None]
    for k in range(1, slot_count):
        holder = owner_ref[covering_ref[0, k]]
        places.append(jnp.clip(holder - me + REACH, 0, 2 * REACH))
        row_offs.append(row_shift_ref[0, k])
        col_offs.append(col_shift_ref[0, k])
        selects.append(jnp.where(row_to - row_from == row_offs[k], 1.0, 0.0).astype(bf16))

    def canvas_block(start, width):
        col = lax.broadcasted_iota(jnp.int32, (1, width), 1) + (start - rim)
        row = lax.broadcasted_iota(jnp.int32, (rows, width), 0)
        total, coverage = None, jnp.ones((rows, width), f32)
        for k in range(slot_count):
            first = margin + start - rim - col_offs[k]
            base = first // LANES if k == 0 else lax.div(first, LANES)
            span = width // LANES + 1
            window = jnp.concatenate([moved[k, base + part] for part in range(span)], axis=1)
            turn = lax.rem(span * LANES - (first - base * LANES), span * LANES)
            placed = pltpu.roll(window, turn, 1)[:, :width]
            total = placed if k == 0 else total + placed
            if k:
                col_old, row_old = col - col_offs[k], row - row_offs[k]
                col_in = jnp.where((col_old >= 0) & (col_old < cols), 1.0, 0.0)
                row_in = jnp.where((row_old >= 0) & (row_old < rows), 1.0, 0.0)
                coverage = coverage + row_in * col_in
        image = jnp.where((col >= 0) & (col < cols), total / coverage, 0.0)
        ext[pl.ds(EDGE, rows), start : start + width] = image.astype(bf16)

    spans = [(chunk * chunk_cols, chunk_cols) for chunk in range(chunks)] + [(cols, LANES)]
    halos = []
    for number, (start, width) in enumerate(spans):
        columns = pl.ds(start, width)
        up = remote(
            ext.at[pl.ds(EDGE, EDGE), columns],
            ext.at[pl.ds(rows + EDGE, EDGE), columns],
            halo_send.at[0, number],
            halo_recv.at[1, number],
            before,
        )
        down = remote(
            ext.at[pl.ds(rows, EDGE), columns],
            ext.at[pl.ds(0, EDGE), columns],
            halo_send.at[1, number],
            halo_recv.at[0, number],
            after,
        )
        halos.append((up, down))

    def canvas_and_halo(number):
        canvas_block(*spans[number])
        pl.when(has_before)(halos[number][0].start)
        pl.when(has_after)(halos[number][1].start)

    def finish_span(number):
        pl.when(has_before)(halos[number][1].wait_recv)
        pl.when(has_after)(halos[number][0].wait_recv)
        start, width = spans[number]
        columns = slice(start, start + width)
        ext_low[:, columns] = ext[:, columns].astype(f32)[8 : rows + 2 * EDGE + 8].astype(bf16)

    for chunk in range(chunks):
        if early + chunk < chunks:
            pass_on(early + chunk)

        @pl.when(has_back)
        def _():
            arrival(back_slot, chunk).wait_recv()
            from_back[chunk].start()

        for slot in (0, 2, 4, 6):
            origin = me + slot - REACH
            pl.when((origin >= 0) & (origin < devices))(arrival(slot, chunk).wait_recv)
        for k in range(1, slot_count):
            product = jnp.dot(selects[k], slots[chunk][places[k]], preferred_element_type=f32)
            for part in range(chunk_cols // LANES):
                moved[k, pad_blocks + chunk * (chunk_cols // LANES) + part] = product[
                    :, part * LANES : (part + 1) * LANES
                ]
        if chunk:
            canvas_and_halo(chunk - 1)
    canvas_and_halo(chunks - 1)
    canvas_and_halo(chunks)

    model_rows = rows + 2 * EDGE
    wide_rows = rows + EDGE
    index = lax.broadcasted_iota(jnp.int32, (wide_rows, LANES), 0)
    low_edge = jnp.where(has_before, 0, psf_rim)
    high_edge = jnp.where(has_after, rows + 2 * psf_rim, rows + psf_rim)
    inside = (index >= low_edge) & (index < high_edge)

    def model_block(block, squares):
        start = pl.multiple_of(block * LANES, LANES)
        window = pl.ds(start, 2 * LANES)
        parts = []
        for step in range(steps):
            if step % 2 == 0:
                parts.append(ext[pl.ds(8 * step, model_rows), window])
            else:
                parts.append(ext_low[pl.ds(8 * (step - 1), model_rows), window])
        product = jnp.dot(
            jnp.concatenate(parts, axis=1), weights[...], preferred_element_type=f32
        )
        for s in range(8):
            y_model[s] = product[:, s * LANES : (s + 1) * LANES]
        first = EDGE - rim - psf_rim
        model = y_model[0, pl.ds(first, wide_rows), :]
        for s in range(1, 8):
            model = model + y_model[s, pl.ds(first + s, wide_rows), :]
        diff = sci_ext[pl.ds(8 - psf_rim, wide_rows), pl.ds(start, LANES)] - model
        diff = jnp.where(inside, diff, 0.0)
        diff_ext[:, pl.ds(start, LANES)] = diff
        own = diff[psf_rim : psf_rim + rows]
        difference_ref[:, pl.ds(start, LANES)] = own
        return squares + jnp.sum((own * own).reshape(rows // 8, 8, LANES), axis=0)

    pl.when(has_before)(sci_down.wait_recv)
    pl.when(has_after)(sci_up.wait_recv)
    ready = chunks // 2
    for number in range(ready):
        finish_span(number)
    first_blocks = ready * chunk_cols // LANES - 1
    squares = lax.fori_loop(0, first_blocks, model_block, jnp.zeros((8, LANES), f32))
    for number in range(ready, chunks + 1):
        finish_span(number)
    partial[...] = lax.fori_loop(first_blocks, blocks, model_block, squares)
    difference_copy = pltpu.make_async_copy(difference_ref, difference_hbm, out_sem.at[0])
    difference_copy.start()
    part_copies = []
    for step in range(1, PIECES):
        part_copies.append(
            remote(partial, partials.at[pos], part_send.at[step - 1], part_recv.at[pos], peer(step))
        )
    for copy in part_copies:
        copy.start()
    partials[pos] = partial[...]

    tail = jnp.zeros((wide_rows, LANES), f32)
    diff_low[...] = pltpu.roll(jnp.concatenate([diff_ext[...], tail], axis=1), psf_rim, 1).astype(bf16)

    def psf_block(block, carry):
        start = pl.multiple_of(block * LANES, LANES)
        product = jnp.dot(
            diff_low[:, pl.ds(start, 2 * LANES)], psf_weights[...], preferred_element_type=f32
        )
        for s in range(psf_taps):
            y_psf[s] = product[:, s * LANES : (s + 1) * LANES]
        response = y_psf[0, pl.ds(0, rows), :]
        for s in range(1, psf_taps):
            response = response + y_psf[s, pl.ds(s, rows), :]
        detection_ref[:, pl.ds(start, LANES)] = response
        return carry

    lax.fori_loop(0, blocks, psf_block, 0)

    for step in range(1, PIECES):
        source = lax.rem(pos + step, PIECES)
        remote(
            partial, partials.at[source], part_send.at[step - 1], part_recv.at[source], peer(step)
        ).wait_recv()
    variance = jnp.sum(jnp.sum(partials[...], axis=0), keepdims=True) / (PIECES * rows * cols)
    detection_ref[...] = detection_ref[...] / jnp.sqrt(variance + 1e-06)
    detection_copy = pltpu.make_async_copy(detection_ref, detection_hbm, out_sem.at[1])
    detection_copy.start()

    for chunk in range(chunks):
        to_beside[chunk].wait_send()
        pl.when(has_far)(to_far[chunk].wait_send)
        to_sibling[chunk].wait_send()
        pl.when(has_onward)(to_onward[chunk].wait_send)
        from_beside[chunk].wait_send()
        pl.when(has_back)(from_back[chunk].wait_send)
    pl.when(has_before)(sci_up.wait_send)
    pl.when(has_after)(sci_down.wait_send)
    for up, down in halos:
        pl.when(has_before)(up.wait_send)
        pl.when(has_after)(down.wait_send)
    difference_copy.wait()
    detection_copy.wait()
    for copy in part_copies:
        copy.wait_send()


def hand_out(difference, detection, difference_out, detection_out):
    difference_out[...] = difference[...]
    detection_out[...] = detection[...]


def shards(
    science,
    template,
    owner_map,
    covering,
    row_shift,
    col_shift,
    basis_cols,
    basis_rows,
    coeffs,
    psf_kernel,
):
    rows, cols = science.shape
    devices = lax.axis_size("visit")
    steps = (basis_cols.shape[1] + 7) // 8
    psf_taps = psf_kernel.shape[0]
    f32, bf16 = jnp.float32, jnp.bfloat16
    hbm = pl.BlockSpec(memory_space=pl.ANY)
    chunks = 4
    slot_count = covering.shape[1]
    wide = cols + LANES
    dma = pltpu.SemaphoreType.DMA
    flops = 2 * cols * (rows + 32) * (2 * LANES) * (8 * steps + psf_taps)
    results = pl.pallas_call(
        functools.partial(kernel, devices),
        out_shape=[jax.ShapeDtypeStruct((rows, cols), f32)] * 2,
        in_specs=[hbm] * 10,
        out_specs=[hbm] * 2,
        scratch_shapes=[
            pltpu.VMEM((rows, cols), f32),
            pltpu.VMEM((rows, cols), f32),
            pltpu.SMEM(owner_map.shape, jnp.int32),
            pltpu.SMEM(covering.shape, jnp.int32),
            pltpu.SMEM(row_shift.shape, jnp.int32),
            pltpu.SMEM(col_shift.shape, jnp.int32),
            pltpu.VMEM(basis_cols.shape, f32),
            pltpu.VMEM(basis_rows.shape, f32),
            pltpu.VMEM(coeffs.shape, f32),
            pltpu.VMEM(psf_kernel.shape, f32),
            pltpu.VMEM((rows, cols), bf16),
            *([pltpu.VMEM((2 * REACH + 1, rows, cols // chunks), bf16)] * chunks),
            pltpu.VMEM((slot_count, cols // LANES + 6, rows, LANES), f32),
            pltpu.VMEM((rows + 3 * EDGE, wide), bf16),
            pltpu.VMEM((rows + 2 * EDGE, wide), bf16),
            pltpu.VMEM((rows + 24, cols), f32),
            pltpu.VMEM((4, LANES, LANES), f32),
            pltpu.VMEM((2, LANES, LANES), f32),
            pltpu.VMEM((steps * 2 * LANES, 8 * LANES), bf16),
            pltpu.VMEM((2 * LANES, psf_taps * LANES), bf16),
            pltpu.VMEM((8, rows + 2 * EDGE, LANES), f32),
            pltpu.VMEM((psf_taps, rows + EDGE, LANES), f32),
            pltpu.VMEM((rows + EDGE, cols), f32),
            pltpu.VMEM((rows + EDGE, wide), bf16),
            pltpu.VMEM((8, LANES), f32),
            pltpu.VMEM((PIECES, 8, LANES), f32),
            dma((10,)),
            dma((3, chunks)),
            dma((2 * REACH + 1, chunks)),
            dma((chunks,)),
            dma((2, chunks)),
            dma((2,)),
            dma((2,)),
            dma((2, chunks + 1)),
            dma((2, chunks + 1)),
            dma((PIECES - 1,)),
            dma((PIECES,)),
            dma((2,)),
        ],
        compiler_params=pltpu.CompilerParams(
            collective_id=0, has_side_effects=True, vmem_limit_bytes=60 * 1024 * 1024
        ),
        cost_estimate=pl.CostEstimate(
            flops=flops, bytes_accessed=rows * cols * 14, transcendentals=0
        ),
    )(
        owner_map,
        covering,
        row_shift,
        col_shift,
        science,
        template,
        basis_cols,
        basis_rows,
        coeffs,
        psf_kernel,
    )
    block = pl.BlockSpec((rows // 4, cols), lambda step: (step, 0))
    return pl.pallas_call(
        hand_out,
        grid=(4,),
        out_shape=[jax.ShapeDtypeStruct((rows, cols), f32)] * 2,
        in_specs=[block] * 2,
        out_specs=[block] * 2,
        compiler_params=pltpu.CompilerParams(vmem_limit_bytes=60 * 1024 * 1024),
        cost_estimate=pl.CostEstimate(flops=0, bytes_accessed=rows * cols * 16, transcendentals=0),
    )(*results)


def solution(mesh):
    return jax.shard_map(
        shards,
        mesh=mesh,
        in_specs=(
            P(("groups", "visit"), None),
            P(("groups", "visit"), None),
            P("groups"),
            P(("groups", "visit"), None),
            P(("groups", "visit"), None),
            P(("groups", "visit"), None),
            P(),
            P(),
            P("groups", None),
            P(),
        ),
        out_specs=(P(("groups", "visit"), None), P(("groups", "visit"), None)),
        check_vma=False,
    )
```
